256 devices in a mesh: views: 16 (over z, x_hi), cols: 16 (over x_lo, y, core).
Axes of the slice: x: 4 (x_hi: 2, x_lo: 2; x = x_hi * 2 + x_lo), y: 4, z: 8, core: 2. Of those that a mesh axis runs over, the one named last changes fastest.
Arguments:
- light_field: bfloat16 [32, 32, 32, 2048], P('views', None, None, 'cols'), may hold values from -6 to 6
Outputs:
- depth_map: float32 [32, 32, 32, 2048], P('views', None, None, 'cols')
The draws below stay inside these ranges and needn't reach their ends.
All inputs are finite; a program needn't handle non-finite values.
Results may differ from the reference program's by a relative error of at most 0.0003.
Values may be sent and summed in bfloat16 or wider, within the bound.
A program may use at most 128 MiB of HBM per device.

```python
import jax
import jax.numpy as jnp
from jax import lax

V = 32
Y = 32
U = 32
X = 2048


def block_levels(rng, shape, shards, low, top_value):
    def one(axis_at, blocks):
        steps = jax.random.uniform(jax.random.fold_in(jax.random.fold_in(rng, 6), axis_at), (blocks,), jnp.float32, low / len(shards), top_value / len(shards))
        return jnp.repeat(jnp.exp(steps), shape[axis_at] // blocks).reshape((-1,) + (1,) * (len(shape) - axis_at - 1))

    factor_of = one(*shards[0])
    for cut in shards[1:]:
        factor_of = factor_of * one(*cut)
    return factor_of


def bell_draw(own_key, dims, scale, reach, pieces=(), held_as=jnp.bfloat16):
    array = scale * jax.random.normal(own_key, dims, jnp.float32)
    if pieces:
        array = array * block_levels(own_key, dims, pieces, -0.22, 0.18)
    return jnp.clip(array, -reach, reach).astype(held_as)


def setup_inputs(seed: int = 0) -> dict:
    keys = jax.random.split(jax.random.key(seed), 2)
    return {
        "light_field": bell_draw(keys[0], (U, V, Y, X), 1.0, 6.0, ((0, 16), (3, 16))),
    }


def shifted(field, axis, step):
    count = field.shape[axis]
    if step == 0:
        return field
    zshape = list(field.shape)
    zshape[axis] = abs(step)
    zeros = jnp.zeros(zshape, field.dtype)
    if step > 0:
        kept = lax.slice_in_dim(field, step, count, axis=axis)
        return jnp.concatenate([kept, zeros], axis=axis)
    kept = lax.slice_in_dim(field, 0, count + step, axis=axis)
    return jnp.concatenate([zeros, kept], axis=axis)

def derivative(field, axis):
    return (shifted(field, axis, 1) - shifted(field, axis, -1)) * 0.5

def smooth(field, axis):
    return 0.25 * shifted(field, axis, -1) + 0.5 * field + 0.25 * shifted(field, axis, 1)

def slope_coherence(first, cross, second):
    slope = -cross / (second + 1.0)
    spread = (second - first) ** 2 + 4.0 * cross * cross
    coherence = spread / ((first + second) ** 2 + 1.0)
    return (slope, coherence)

def plane_fields(field, axis_a, axis_b):
    grad_a = derivative(field, axis_a)
    grad_b = derivative(field, axis_b)
    parts = [smooth(smooth(c, axis_a), axis_b) for c in (grad_a * grad_a, grad_a * grad_b, grad_b * grad_b)]
    return slope_coherence(parts[0], parts[1], parts[2])

def reference(light_field):

    def horizontal(plane):
        return jnp.stack(plane_fields(plane.astype(jnp.float32), 0, 2))

    def vertical(plane):
        return jnp.stack(plane_fields(plane.astype(jnp.float32), 0, 1))
    flat_fields = lax.map(horizontal, light_field)
    upright = lax.map(vertical, jnp.moveaxis(light_field, 1, 0))

    def finish(inputs):
        flat_pair, upright_pair = inputs
        joined = (flat_pair[1] * flat_pair[0] + upright_pair[1] * upright_pair[0]) / (flat_pair[1] + upright_pair[1] + 0.1)
        step_x = shifted(joined, 2, 1) - joined
        step_y = shifted(joined, 1, 1) - joined
        scale = jnp.sqrt(step_x * step_x + step_y * step_y + 1.0)
        flux_x = step_x / scale
        flux_y = step_y / scale
        spread = flux_x - shifted(flux_x, 2, -1) + flux_y - shifted(flux_y, 1, -1)
        return joined + 0.2 * spread
    upright_rows = jnp.transpose(upright, (2, 1, 0, 3, 4))
    return lax.map(finish, (flat_fields, upright_rows))
```

```python
import functools

import jax
import jax.numpy as jnp
from jax import lax
from jax.experimental import pallas as pl
from jax.experimental.pallas import tpu as pltpu
from jax.sharding import PartitionSpec as P

MESH = pl.DeviceIdType.MESH
F32 = jnp.float32
BF16 = jnp.bfloat16
ROWS, V, Y, X = 2, 32, 32, 128
CHUNK = 4
CHUNKS = V // CHUNK
STEP = 2
PLANE = V * Y


def recip(x):
    r = pl.reciprocal(x, approx=True)
    return r * (2.0 - x * r)


def measures(first, cross, second):
    apart = second - first
    whole = second + first
    twice = cross + cross
    return apart * apart + twice * twice, whole * whole + 4096.0, cross, second + 64.0


def weighted(first, cross, second):
    spread, energy, cross, pivot = measures(first, cross, second)
    part = spread * recip(energy * pivot)
    return part * pivot + 0.1, part * cross


def join(weight_h, moment_h, first, cross, second):
    spread, energy, cross, pivot = measures(first, cross, second)
    above = moment_h * (energy * pivot) + spread * cross
    below = pivot * (energy * weight_h + spread)
    return -(above * recip(below))


def kernel(
    nv,
    nc,
    f_hbm,
    o_hbm,
    fv,
    full,
    got,
    wide,
    weight,
    moment,
    fix,
    out,
    pack,
    pack_l,
    pack_r,
    mid,
    mids,
    edge,
    edge_j,
    edge_d,
    load_sem,
    near_s,
    near_r,
    far_s,
    far_r,
    pack_s,
    pack_rs,
    mid_s,
    mid_r,
    out_s,
):
    vi = lax.axis_index("views")
    cj = lax.axis_index("cols")
    odd = lax.rem(vi, 2)
    even = 1 - odd
    partner = vi + 1 - 2 * odd
    ahead = lax.rem(vi + nv + 2 - 4 * odd, nv)
    behind = lax.rem(vi + nv - 2 + 4 * odd, nv)
    left = lax.rem(cj + nc - 1, nc)
    right = lax.rem(cj + 1, nc)
    at_top = vi == 0
    at_bottom = vi == nv - 1
    has_far = jnp.logical_and(vi > 0, vi < nv - 1)
    sends_far = jnp.logical_and(vi != nv - 2, vi != 1)

    barrier = pltpu.get_barrier_semaphore()
    for there in ((partner, cj), (behind, cj), (vi, left), (vi, right)):
        pl.semaphore_signal(barrier, inc=1, device_id=there, device_id_type=MESH)

    load = pltpu.make_async_copy(f_hbm, fv, load_sem)
    load.start()
    load.wait()

    row8 = lax.broadcasted_iota(jnp.int32, (8, PLANE), 0)
    row16 = lax.broadcasted_iota(jnp.int32, (16, X), 0)
    lane16 = lax.broadcasted_iota(jnp.int32, (16, X), 1)
    r8 = lax.rem(row16, 8)
    wanted = jnp.where(r8 < 4, r8 + (X - 4), r8 - 4)

    packed = jnp.zeros((16, PLANE), F32)
    for u in range(ROWS):
        pick = jnp.where(jnp.logical_and(lane16 == wanted, row16 // 8 == u), 1.0, 0.0).astype(BF16)
        packed = packed + lax.dot_general(
            pick, fv[u].reshape(PLANE, X), (((1,), (1,)), ((), ())), preferred_element_type=F32
        )
    pack[...] = packed.astype(BF16)

    pl.semaphore_wait(barrier, 4)

    def remote(src, dst, s, r, there):
        return pltpu.make_async_remote_copy(
            src_ref=src, dst_ref=dst, send_sem=s, recv_sem=r, device_id=there, device_id_type=MESH
        )

    def near(k):
        span = pl.ds(k * CHUNK, CHUNK)
        return remote(fv.at[:, span], got.at[odd, :, span], near_s.at[k], near_r.at[k], (partner, cj))

    def near_in(k):
        span = pl.ds(k * CHUNK, CHUNK)
        return remote(fv.at[:, span], got.at[even, :, span], near_s.at[k], near_r.at[k], (partner, cj))

    def far(k):
        span = pl.ds(k * CHUNK, CHUNK)
        return remote(got.at[even, :, span], got.at[odd, :, span], far_s.at[k], far_r.at[k], (ahead, cj))

    to_left = remote(pack, pack_r, pack_s.at[0], pack_rs.at[0], (vi, left))
    to_right = remote(pack, pack_l, pack_s.at[1], pack_rs.at[1], (vi, right))
    to_left.start()
    to_right.start()
    for k in range(CHUNKS):
        near(k).start()

    @pl.when(at_top)
    def _():
        got[0, 0] = fv[0]
        got[0, 1] = jnp.zeros((V, Y, X), BF16)

    @pl.when(at_bottom)
    def _():
        got[1, 0] = jnp.zeros((V, Y, X), BF16)
        got[1, 1] = fv[1]

    def lanes(a, k):
        return pltpu.roll(a, (-k) % a.shape[-1], a.ndim - 1)

    def smooth_lanes(a):
        pair = a + lanes(a, -1)
        return pair + lanes(pair, 1)

    def horizontal(i, carry):
        u = i // 2
        rows = pl.ds(pl.multiple_of(lax.rem(i, 2) * 16, 16), 16)
        nothing = jnp.zeros((16, X), F32)
        field = [fv[u, v, rows, :].astype(F32) for v in range(V)]
        for v in range(V):
            full[u, v, rows, :] = field[v]
        pairs, last = None, (nothing,) * 3
        for v in range(V + 1):
            if v < V:
                grad_v = (field[v + 1] if v + 1 < V else nothing) - (field[v - 1] if v else nothing)
                grad_x = lanes(field[v], 1) - lanes(field[v], -1)
                now = tuple(smooth_lanes(c) for c in (grad_v * grad_v, grad_v * grad_x, grad_x * grad_x))
            else:
                now = (nothing,) * 3
            sums = tuple(a + b for a, b in zip(last, now))
            if v:
                w, m = weighted(*(a + b for a, b in zip(pairs, sums)))
                weight[u, v - 1, rows, :] = w
                moment[u, v - 1, rows, :] = m
            pairs, last = sums, now
        return carry

    lax.fori_loop(0, 2, horizontal, 0)

    to_left.wait_recv()
    to_right.wait_recv()
    first, final = cj == 0, cj == nc - 1
    own = pack[...].astype(F32)
    from_l = pack_l[...].astype(F32)
    from_r = pack_r[...].astype(F32)
    mixed = []
    for u in range(ROWS):
        mine = own[8 * u : 8 * u + 8]
        l_in = from_l[8 * u : 8 * u + 8]
        r_in = from_r[8 * u : 8 * u + 8]
        flip_l = jnp.where(row8 == 2, pltpu.roll(mine, 6, 0), 0.0)
        flip_r = jnp.where(row8 == 5, pltpu.roll(mine, 2, 0), 0.0)
        l_in = jnp.where(first, flip_l, l_in)
        r_in = jnp.where(final, flip_r, r_in)
        e_l = jnp.where(row8 < 4, l_in, mine)
        e_r = jnp.where(row8 < 4, mine, r_in)
        edge[0, 2 + u] = e_l
        edge[1, 2 + u] = e_r
        mixed.append(jnp.where(jnp.logical_and(row8 >= 2, row8 < 6), e_l, pltpu.roll(e_r, 4, 0)))
    mid[...] = jnp.concatenate(mixed, axis=0).astype(BF16)
    mid_near = remote(mid, mids.at[odd], mid_s.at[0], mid_r.at[0], (partner, cj))
    mid_near_in = remote(mid, mids.at[even], mid_s.at[0], mid_r.at[0], (partner, cj))
    mid_far = remote(mids.at[even], mids.at[odd], mid_s.at[1], mid_r.at[1], (ahead, cj))
    mid_near.start()

    lax.fori_loop(2, 4, horizontal, 0)

    mid_near_in.wait_recv()

    @pl.when(sends_far)
    def _():
        mid_far.start()

    near_in(0).wait_recv()

    @pl.when(sends_far)
    def _():
        far(0).start()

    @pl.when(has_far)
    def _():
        mid_far.wait_recv()

    for slot in range(2):
        rows_in = mids[slot].astype(F32)
        for u in range(ROWS):
            tile = rows_in[8 * u : 8 * u + 8]
            edge[0, 4 * slot + u] = tile
            edge[1, 4 * slot + u] = pltpu.roll(tile, 4, 0)

    @pl.when(at_top)
    def _():
        for side in range(2):
            edge[side, 0] = edge[side, 2]
            edge[side, 1] = jnp.zeros((8, PLANE), F32)

    @pl.when(at_bottom)
    def _():
        for side in range(2):
            edge[side, 4] = jnp.zeros((8, PLANE), F32)
            edge[side, 5] = edge[side, 3]

    place = lax.broadcasted_iota(jnp.int32, (8, PLANE), 1)
    y_at = lax.rem(place, Y)

    def cols_by(a, k):
        return pltpu.roll(a, (-k) % 8, 0)

    def y_by(a, k):
        return jnp.where(y_at == (Y - 1 if k > 0 else 0), 0.0, pltpu.roll(a, (-k) % PLANE, 1))

    def v_by(a, k):
        return jnp.where(
            place >= PLANE - Y if k > 0 else place < Y, 0.0, pltpu.roll(a, (-k * Y) % PLANE, 1)
        )

    def smooth_by(by, a):
        return by(a, -1) + (a + a) + by(a, 1)

    def edges(side, carry):
        j_below = jnp.where(jnp.logical_and(final, side == 1), 4, 8)
        q_from = jnp.where(jnp.logical_and(first, side == 0), 4, 0)
        tiles = [edge[side, r] for r in range(6)]
        comps = []
        for r in range(1, 5):
            grad_u = tiles[r + 1] - tiles[r - 1]
            grad_y = y_by(tiles[r], 1) - y_by(tiles[r], -1)
            comps.append((grad_u * grad_u, grad_u * grad_y, grad_y * grad_y))
        for u in range(ROWS):
            f = tiles[2 + u]
            grad_v = v_by(f, 1) - v_by(f, -1)
            grad_x = cols_by(f, 1) - cols_by(f, -1)
            w, m = weighted(
                *(
                    smooth_by(v_by, smooth_by(cols_by, c))
                    for c in (grad_v * grad_v, grad_v * grad_x, grad_x * grad_x)
                )
            )
            tensor = [
                smooth_by(y_by, a + (b + b) + c) for a, b, c in zip(comps[u], comps[u + 1], comps[u + 2])
            ]
            joined = jnp.where(row8 < j_below, join(w, m, *tensor), 0.0)
            step_x = cols_by(joined, 1) - joined
            step_y = y_by(joined, 1) - joined
            scale = lax.rsqrt(step_x * step_x + step_y * step_y + 1.0)
            flux_x = jnp.where(row8 >= q_from, step_x * scale, 0.0)
            flux_y = step_y * scale
            depth = joined + 0.2 * (flux_x - cols_by(flux_x, -1) + flux_y - y_by(flux_y, -1))
            edge_j[side, u] = pltpu.roll(joined, 4, 0)
            edge_d[side, u] = pltpu.roll(depth, 5, 0)
        return carry

    lax.fori_loop(0, 2, edges, 0)

    small = lax.broadcasted_iota(jnp.int32, (8, X), 0)

    def spread_out(u, carry):
        for b in range(PLANE // X):
            part = pl.ds(b * X, X)
            both = jnp.where(small == 0, edge_d[1, u, :, part], edge_d[0, u, :, part])
            block = jnp.concatenate(
                [
                    edge_j[0, u, :, part],
                    jnp.zeros((56, X), F32),
                    both,
                    jnp.zeros((48, X), F32),
                    edge_j[1, u, :, part],
                ],
                axis=0,
            )
            fix[u, pl.ds(4 * b, 4)] = block.T.reshape(4, Y, X)
        return carry

    lax.fori_loop(0, 2, spread_out, 0)

    lane = lax.broadcasted_iota(jnp.int32, (STEP, 8, X), 2)
    sub = lax.broadcasted_iota(jnp.int32, (STEP, 8, X), 1)
    rim = jnp.logical_or(lane < 2, lane >= X - 2)
    outer = jnp.logical_or(lane == 0, lane == X - 1)

    def parts(ref, *at):
        return [ref[(*at, pl.ds(p, 8, stride=4), slice(None))] for p in range(4)]

    def y_up(a, rest=0.0):
        return a[1:] + [jnp.where(sub == 7, rest, pltpu.roll(a[0], 7, 1))]

    def y_down(a):
        return [jnp.where(sub == 0, 0.0, pltpu.roll(a[3], 1, 1))] + a[:3]

    def smooth_y(a):
        pair = [b + c for b, c in zip(a, y_down(a))]
        return [b + c for b, c in zip(pair, y_up(pair, a[3]))]

    def vertical(v0):
        span = pl.ds(v0, STEP)
        for slot in range(2):
            for u in range(ROWS):
                wide[2 * slot + u] = got[slot, u, span].astype(F32)
        every = slice(None)
        field = (
            [parts(wide, 0, every), parts(wide, 1, every)]
            + [parts(full, u, span) for u in range(ROWS)]
            + [parts(wide, 2, every), parts(wide, 3, every)]
        )
        comps = []
        for r in range(1, 5):
            grad_u = [a - b for a, b in zip(field[r + 1], field[r - 1])]
            grad_y = [a - b for a, b in zip(y_up(field[r]), y_down(field[r]))]
            comps.append(
                [
                    [a * b for a, b in zip(g, h)]
                    for g, h in ((grad_u, grad_u), (grad_u, grad_y), (grad_y, grad_y))
                ]
            )
        pairs = [
            [[a + b for a, b in zip(c, d)] for c, d in zip(comps[r], comps[r + 1])] for r in range(3)
        ]
        for u in range(ROWS):
            tensor = [
                smooth_y([a + b for a, b in zip(c, d)]) for c, d in zip(pairs[u], pairs[u + 1])
            ]
            w, m, t = parts(weight, u, span), parts(moment, u, span), parts(fix, u, span)
            joined = [
                jnp.where(rim, t[p], join(w[p], m[p], *(c[p] for c in tensor))) for p in range(4)
            ]
            flux_x, flux_y = [], []
            for here, below in zip(joined, y_up(joined)):
                step_x = lanes(here, 1) - here
                step_y = below - here
                scale = lax.rsqrt(step_x * step_x + step_y * step_y + 1.0)
                flux_x.append(step_x * scale)
                flux_y.append(step_y * scale)
            for p, above in enumerate(y_down(flux_y)):
                depth = joined[p] + 0.2 * (flux_x[p] - lanes(flux_x[p], -1) + flux_y[p] - above)
                out[u, span, pl.ds(p, 8, stride=4), :] = jnp.where(outer, lanes(t[p], -63), depth)

    def stored(k):
        span = pl.ds(k * CHUNK, CHUNK)
        return pltpu.make_async_copy(out.at[:, span], o_hbm.at[:, span], out_s.at[k])

    def chunk(k, carry):
        @pl.when(k + 1 < CHUNKS)
        def _():
            near_in(k + 1).wait_recv()

            @pl.when(sends_far)
            def _():
                far(k + 1).start()

        @pl.when(has_far)
        def _():
            far(k).wait_recv()

        def inner(i, c):
            vertical(k * CHUNK + i * STEP)
            return c

        lax.fori_loop(0, CHUNK // STEP, inner, 0)
        stored(k).start()
        return carry

    lax.fori_loop(0, CHUNKS, chunk, 0)

    to_left.wait_send()
    to_right.wait_send()
    mid_near.wait_send()
    for k in range(CHUNKS):
        near(k).wait_send()

    @pl.when(sends_far)
    def _():
        mid_far.wait_send()
        for k in range(CHUNKS):
            far(k).wait_send()

    for k in range(CHUNKS):
        stored(k).wait()


def local(nv, nc, light_field):
    block = (ROWS, V, Y, X)
    dma = pltpu.SemaphoreType.DMA
    return pl.pallas_call(
        functools.partial(kernel, nv, nc),
        out_shape=jax.ShapeDtypeStruct(block, F32),
        in_specs=[pl.BlockSpec(memory_space=pl.ANY)],
        out_specs=pl.BlockSpec(memory_space=pl.ANY),
        scratch_shapes=[
            pltpu.VMEM(block, BF16),
            pltpu.VMEM(block, F32),
            pltpu.VMEM((2, *block), BF16),
            pltpu.VMEM((4, STEP, Y, X), F32),
            pltpu.VMEM(block, F32),
            pltpu.VMEM(block, F32),
            pltpu.VMEM(block, F32),
            pltpu.VMEM(block, F32),
            pltpu.VMEM((16, PLANE), BF16),
            pltpu.VMEM((16, PLANE), BF16),
            pltpu.VMEM((16, PLANE), BF16),
            pltpu.VMEM((16, PLANE), BF16),
            pltpu.VMEM((2, 16, PLANE), BF16),
            pltpu.VMEM((2, 6, 8, PLANE), F32),
            pltpu.VMEM((2, ROWS, 8, PLANE), F32),
            pltpu.VMEM((2, ROWS, 8, PLANE), F32),
            dma,
            dma((CHUNKS,)),
            dma((CHUNKS,)),
            dma((CHUNKS,)),
            dma((CHUNKS,)),
            dma((2,)),
            dma((2,)),
            dma((2,)),
            dma((2,)),
            dma((CHUNKS,)),
        ],
        compiler_params=pltpu.CompilerParams(
            collective_id=0, has_side_effects=True, vmem_limit_bytes=32 << 20
        ),
        cost_estimate=pl.CostEstimate(flops=60_000_000, bytes_accessed=1_600_000, transcendentals=800_000),
    )(light_field)


def solution(mesh):
    return jax.shard_map(
        functools.partial(local, mesh.shape["views"], mesh.shape["cols"]),
        mesh=mesh,
        in_specs=(P("views", None, None, "cols"),),
        out_specs=P("views", None, None, "cols"),
        check_vma=False,
    )
```

```python
import functools

import jax
import jax.numpy as jnp
from jax import lax
from jax.experimental import pallas as pl
from jax.experimental.pallas import tpu as pltpu
from jax.sharding import PartitionSpec as P

MESH = pl.DeviceIdType.MESH
F32 = jnp.float32
BF16 = jnp.bfloat16
ROWS, V, Y, X = 2, 32, 32, 128
CHUNK = 4
CHUNKS = V // CHUNK
STEP = 4
H_CHUNK = 8
H_STEPS = V // H_CHUNK
AHEAD = 3
FIRST = 3
PLANE = V * Y


def recip(x):
    r = pl.reciprocal(x, approx=True)
    return r * (2.0 - x * r)


def measures(first, cross, second):
    apart = second - first
    whole = second + first
    twice = cross + cross
    return apart * apart + twice * twice, whole * whole + 4096.0, cross, second + 64.0


def weighted(first, cross, second):
    spread, energy, cross, pivot = measures(first, cross, second)
    part = spread * recip(energy * pivot)
    return part * pivot + 0.1, part * cross


def join(weight_h, moment_h, first, cross, second):
    spread, energy, cross, pivot = measures(first, cross, second)
    above = moment_h * (energy * pivot) + spread * cross
    below = pivot * (energy * weight_h + spread)
    return -(above * recip(below))


def kernel(
    nv,
    nc,
    f_hbm,
    out,
    fv,
    full,
    got,
    wide,
    weight,
    moment,
    fix,
    pack,
    pack_l,
    pack_r,
    mid,
    mids,
    edge,
    edge_j,
    edge_d,
    load_sem,
    near_s,
    near_r,
    far_s,
    far_r,
    pack_s,
    pack_rs,
    mid_s,
    mid_r,
):
    vi = lax.axis_index("views")
    cj = lax.axis_index("cols")
    odd = lax.rem(vi, 2)
    even = 1 - odd
    partner = vi + 1 - 2 * odd
    ahead = lax.rem(vi + nv + 2 - 4 * odd, nv)
    behind = lax.rem(vi + nv - 2 + 4 * odd, nv)
    left = lax.rem(cj + nc - 1, nc)
    right = lax.rem(cj + 1, nc)
    at_top = vi == 0
    at_bottom = vi == nv - 1
    has_far = jnp.logical_and(vi > 0, vi < nv - 1)
    sends_far = jnp.logical_and(vi != nv - 2, vi != 1)

    barrier = pltpu.get_barrier_semaphore()
    for there in ((partner, cj), (behind, cj), (vi, left), (vi, right)):
        pl.semaphore_signal(barrier, inc=1, device_id=there, device_id_type=MESH)

    load = pltpu.make_async_copy(f_hbm, fv, load_sem)
    load.start()
    load.wait()

    row8 = lax.broadcasted_iota(jnp.int32, (8, PLANE), 0)
    row16 = lax.broadcasted_iota(jnp.int32, (16, X), 0)
    lane16 = lax.broadcasted_iota(jnp.int32, (16, X), 1)
    r8 = lax.rem(row16, 8)
    wanted = jnp.where(r8 < 4, r8 + (X - 4), r8 - 4)

    packed = jnp.zeros((16, PLANE), F32)
    for u in range(ROWS):
        pick = jnp.where(jnp.logical_and(lane16 == wanted, row16 // 8 == u), 1.0, 0.0).astype(BF16)
        packed = packed + lax.dot_general(
            pick, fv[u].reshape(PLANE, X), (((1,), (1,)), ((), ())), preferred_element_type=F32
        )
    pack[...] = packed.astype(BF16)

    pl.semaphore_wait(barrier, 4)

    def remote(src, dst, s, r, there):
        return pltpu.make_async_remote_copy(
            src_ref=src, dst_ref=dst, send_sem=s, recv_sem=r, device_id=there, device_id_type=MESH
        )

    def near(k):
        span = pl.ds(k * CHUNK, CHUNK)
        return remote(fv.at[:, span], got.at[odd, :, span], near_s.at[k], near_r.at[k], (partner, cj))

    def near_in(k):
        span = pl.ds(k * CHUNK, CHUNK)
        return remote(fv.at[:, span], got.at[even, :, span], near_s.at[k], near_r.at[k], (partner, cj))

    def far(k):
        span = pl.ds(k * CHUNK, CHUNK)
        return remote(got.at[even, :, span], got.at[odd, :, span], far_s.at[k], far_r.at[k], (ahead, cj))

    to_left = remote(pack, pack_r, pack_s.at[0], pack_rs.at[0], (vi, left))
    to_right = remote(pack, pack_l, pack_s.at[1], pack_rs.at[1], (vi, right))
    to_left.start()
    to_right.start()
    for k in range(FIRST):
        near(k).start()

    @pl.when(at_top)
    def _():
        got[0, 0] = fv[0]
        got[0, 1] = jnp.zeros((V, Y, X), BF16)

    @pl.when(at_bottom)
    def _():
        got[1, 0] = jnp.zeros((V, Y, X), BF16)
        got[1, 1] = fv[1]

    def lanes(a, k):
        return pltpu.roll(a, (-k) % a.shape[-1], a.ndim - 1)

    def smooth_lanes(a):
        pair = a + lanes(a, -1)
        return pair + lanes(pair, 1)

    def horizontal(i, carry):
        before, last = carry
        u = i // H_STEPS
        v0 = lax.rem(i, H_STEPS) * H_CHUNK
        top = v0 == 0
        before = [jnp.where(top, 0.0, c) for c in before]
        last = [jnp.where(top, 0.0, c) for c in last]
        here = fv[u, pl.ds(v0, H_CHUNK)].astype(F32)
        full[u, pl.ds(v0, H_CHUNK)] = here
        above = jnp.where(top, 0.0, fv[u, jnp.maximum(v0 - 1, 0)].astype(F32))
        below = jnp.where(
            v0 + H_CHUNK < V, fv[u, jnp.minimum(v0 + H_CHUNK, V - 1)].astype(F32), 0.0
        )
        mid_x = jnp.concatenate([above[None], here, below[None]], 0)
        left_x, right_x = lanes(mid_x, -1), lanes(mid_x, 1)
        grad_v = [a[2:] - a[:-2] for a in (left_x, mid_x, right_x)]
        grad_x = [here - lanes(here, -2), right_x[1:-1] - left_x[1:-1], lanes(here, 2) - here]

        def smooth_x(p, q):
            a, b, c = (s * t for s, t in zip(p, q))
            return (a + c) + (b + b)

        now = [smooth_x(grad_v, grad_v), smooth_x(grad_v, grad_x), smooth_x(grad_x, grad_x)]
        run = [jnp.concatenate([a[None], b[None], c], 0) for a, b, c in zip(before, last, now)]
        pairs = [c[1:] + c[:-1] for c in run]
        w, m = weighted(*(c[1:] + c[:-1] for c in pairs))
        weight[u, pl.ds(v0, H_CHUNK)] = w
        moment[u, pl.ds(v0, H_CHUNK)] = m

        @pl.when(v0 == V - H_CHUNK)
        def _():
            w, m = weighted(*(c[-1] + d[-1] for c, d in zip(pairs, now)))
            weight[u, V] = w
            moment[u, V] = m

        return [c[H_CHUNK - 2] for c in now], [c[H_CHUNK - 1] for c in now]

    zeros = [jnp.zeros((Y, X), F32)] * 3
    lax.fori_loop(0, H_STEPS, horizontal, (zeros, zeros))

    to_left.wait_recv()
    to_right.wait_recv()
    first, final = cj == 0, cj == nc - 1
    own = pack[...].astype(F32)
    from_l = pack_l[...].astype(F32)
    from_r = pack_r[...].astype(F32)
    mixed = []
    for u in range(ROWS):
        mine = own[8 * u : 8 * u + 8]
        l_in = from_l[8 * u : 8 * u + 8]
        r_in = from_r[8 * u : 8 * u + 8]
        flip_l = jnp.where(row8 == 2, pltpu.roll(mine, 6, 0), 0.0)
        flip_r = jnp.where(row8 == 5, pltpu.roll(mine, 2, 0), 0.0)
        l_in = jnp.where(first, flip_l, l_in)
        r_in = jnp.where(final, flip_r, r_in)
        e_l = jnp.where(row8 < 4, l_in, mine)
        e_r = jnp.where(row8 < 4, mine, r_in)
        edge[0, 2 + u] = e_l
        edge[1, 2 + u] = e_r
        mixed.append(jnp.where(jnp.logical_and(row8 >= 2, row8 < 6), e_l, pltpu.roll(e_r, 4, 0)))
    mid[...] = jnp.concatenate(mixed, axis=0).astype(BF16)
    mid_near = remote(mid, mids.at[odd], mid_s.at[0], mid_r.at[0], (partner, cj))
    mid_near_in = remote(mid, mids.at[even], mid_s.at[0], mid_r.at[0], (partner, cj))
    mid_far = remote(mids.at[even], mids.at[odd], mid_s.at[1], mid_r.at[1], (ahead, cj))
    mid_near.start()
    for k in range(FIRST, CHUNKS):
        near(k).start()

    def relay(k):
        near_in(k).wait_recv()

        @pl.when(sends_far)
        def _():
            far(k).start()

    lax.fori_loop(H_STEPS, 2 * H_STEPS, horizontal, (zeros, zeros))

    relay(0)
    relay(1)
    mid_near_in.wait_recv()

    @pl.when(sends_far)
    def _():
        mid_far.start()

    relay(2)

    @pl.when(has_far)
    def _():
        mid_far.wait_recv()

    for slot in range(2):
        rows_in = mids[slot].astype(F32)
        for u in range(ROWS):
            tile = rows_in[8 * u : 8 * u + 8]
            edge[0, 4 * slot + u] = tile
            edge[1, 4 * slot + u] = pltpu.roll(tile, 4, 0)

    @pl.when(at_top)
    def _():
        for side in range(2):
            edge[side, 0] = edge[side, 2]
            edge[side, 1] = jnp.zeros((8, PLANE), F32)

    @pl.when(at_bottom)
    def _():
        for side in range(2):
            edge[side, 4] = jnp.zeros((8, PLANE), F32)
            edge[side, 5] = edge[side, 3]

    place = lax.broadcasted_iota(jnp.int32, (8, PLANE), 1)
    y_at = lax.rem(place, Y)

    def cols_by(a, k):
        return pltpu.roll(a, (-k) % 8, 0)

    def y_by(a, k):
        return jnp.where(y_at == (Y - 1 if k > 0 else 0), 0.0, pltpu.roll(a, (-k) % PLANE, 1))

    def v_by(a, k):
        return jnp.where(
            place >= PLANE - Y if k > 0 else place < Y, 0.0, pltpu.roll(a, (-k * Y) % PLANE, 1)
        )

    def smooth_by(by, a):
        return by(a, -1) + (a + a) + by(a, 1)

    def edges(side, carry):
        j_below = jnp.where(jnp.logical_and(final, side == 1), 4, 8)
        q_from = jnp.where(jnp.logical_and(first, side == 0), 4, 0)
        tiles = [edge[side, r] for r in range(6)]
        comps = []
        for r in range(1, 5):
            grad_u = tiles[r + 1] - tiles[r - 1]
            grad_y = y_by(tiles[r], 1) - y_by(tiles[r], -1)
            comps.append((grad_u * grad_u, grad_u * grad_y, grad_y * grad_y))
        for u in range(ROWS):
            f = tiles[2 + u]
            grad_v = v_by(f, 1) - v_by(f, -1)
            grad_x = cols_by(f, 1) - cols_by(f, -1)
            w, m = weighted(
                *(
                    smooth_by(v_by, smooth_by(cols_by, c))
                    for c in (grad_v * grad_v, grad_v * grad_x, grad_x * grad_x)
                )
            )
            tensor = [
                smooth_by(y_by, a + (b + b) + c) for a, b, c in zip(comps[u], comps[u + 1], comps[u + 2])
            ]
            joined = jnp.where(row8 < j_below, join(w, m, *tensor), 0.0)
            step_x = cols_by(joined, 1) - joined
            step_y = y_by(joined, 1) - joined
            scale = lax.rsqrt(step_x * step_x + step_y * step_y + 1.0)
            flux_x = jnp.where(row8 >= q_from, step_x * scale, 0.0)
            flux_y = step_y * scale
            depth = joined + 0.2 * (flux_x - cols_by(flux_x, -1) + flux_y - y_by(flux_y, -1))
            edge_j[side, u] = pltpu.roll(joined, 4, 0)
            edge_d[side, u] = pltpu.roll(depth, 5, 0)
        relay(3 + side)
        return carry

    lax.fori_loop(0, 2, edges, 0)

    small = lax.broadcasted_iota(jnp.int32, (8, X), 0)

    def spread_out(u, carry):
        for b in range(PLANE // X):
            part = pl.ds(b * X, X)
            both = jnp.where(small == 0, edge_d[1, u, :, part], edge_d[0, u, :, part])
            block = jnp.concatenate(
                [
                    edge_j[0, u, :, part],
                    jnp.zeros((56, X), F32),
                    both,
                    jnp.zeros((48, X), F32),
                    edge_j[1, u, :, part],
                ],
                axis=0,
            )
            fix[u, pl.ds(4 * b, 4)] = block.T.reshape(4, Y, X)
        return carry

    lax.fori_loop(0, 2, spread_out, 0)

    lane = lax.broadcasted_iota(jnp.int32, (STEP, 8, X), 2)
    sub = lax.broadcasted_iota(jnp.int32, (STEP, 8, X), 1)
    rim = jnp.logical_or(lane < 2, lane >= X - 2)
    outer = jnp.logical_or(lane == 0, lane == X - 1)

    def parts(ref, *at):
        return [ref[(*at, pl.ds(p, 8, stride=4), slice(None))] for p in range(4)]

    def y_up(a, rest=0.0):
        return a[1:] + [jnp.where(sub == 7, rest, pltpu.roll(a[0], 7, 1))]

    def y_down(a):
        return [jnp.where(sub == 0, 0.0, pltpu.roll(a[3], 1, 1))] + a[:3]

    def smooth_y(a):
        pair = [b + c for b, c in zip(a, y_down(a))]
        return [b + c for b, c in zip(pair, y_up(pair, a[3]))]

    def vertical(v0):
        span = pl.ds(v0, STEP)
        for slot in range(2):
            for u in range(ROWS):
                wide[2 * slot + u] = got[slot, u, span].astype(F32)
        every = slice(None)
        field = (
            [parts(wide, 0, every), parts(wide, 1, every)]
            + [parts(full, u, span) for u in range(ROWS)]
            + [parts(wide, 2, every), parts(wide, 3, every)]
        )
        comps = []
        for r in range(1, 5):
            grad_u = [a - b for a, b in zip(field[r + 1], field[r - 1])]
            grad_y = [a - b for a, b in zip(y_up(field[r]), y_down(field[r]))]
            comps.append(
                [
                    [a * b for a, b in zip(g, h)]
                    for g, h in ((grad_u, grad_u), (grad_u, grad_y), (grad_y, grad_y))
                ]
            )
        pairs = [
            [[a + b for a, b in zip(c, d)] for c, d in zip(comps[r], comps[r + 1])] for r in range(3)
        ]
        for u in range(ROWS):
            tensor = [
                smooth_y([a + b for a, b in zip(c, d)]) for c, d in zip(pairs[u], pairs[u + 1])
            ]
            past = pl.ds(v0 + 1, STEP)
            w, m, t = parts(weight, u, past), parts(moment, u, past), parts(fix, u, span)
            joined = [
                jnp.where(rim, t[p], join(w[p], m[p], *(c[p] for c in tensor))) for p in range(4)
            ]
            flux_x, flux_y = [], []
            for here, below in zip(joined, y_up(joined)):
                step_x = lanes(here, 1) - here
                step_y = below - here
                scale = lax.rsqrt(step_x * step_x + step_y * step_y + 1.0)
                flux_x.append(step_x * scale)
                flux_y.append(step_y * scale)
            for p, above in enumerate(y_down(flux_y)):
                depth = joined[p] + 0.2 * (flux_x[p] - lanes(flux_x[p], -1) + flux_y[p] - above)
                out[u, span, pl.ds(p, 8, stride=4), :] = jnp.where(outer, lanes(t[p], -63), depth)

    def chunk(k, carry):
        @pl.when(jnp.logical_and(k >= 5 - AHEAD, k + AHEAD < CHUNKS))
        def _():
            relay(k + AHEAD)

        @pl.when(has_far)
        def _():
            far(k).wait_recv()

        def inner(i, c):
            vertical(k * CHUNK + i * STEP)
            return c

        lax.fori_loop(0, CHUNK // STEP, inner, 0)
        return carry

    lax.fori_loop(0, CHUNKS, chunk, 0)

    to_left.wait_send()
    to_right.wait_send()
    mid_near.wait_send()
    for k in range(CHUNKS):
        near(k).wait_send()

    @pl.when(sends_far)
    def _():
        mid_far.wait_send()
        for k in range(CHUNKS):
            far(k).wait_send()


def local(nv, nc, light_field):
    block = (ROWS, V, Y, X)
    dma = pltpu.SemaphoreType.DMA
    return pl.pallas_call(
        functools.partial(kernel, nv, nc),
        out_shape=jax.ShapeDtypeStruct(block, F32),
        in_specs=[pl.BlockSpec(memory_space=pltpu.HBM)],
        out_specs=pl.BlockSpec(memory_space=pltpu.VMEM),
        scratch_shapes=[
            pltpu.VMEM(block, BF16),
            pltpu.VMEM(block, F32),
            pltpu.VMEM((2, *block), BF16),
            pltpu.VMEM((4, STEP, Y, X), F32),
            pltpu.VMEM((ROWS, V + 1, Y, X), F32),
            pltpu.VMEM((ROWS, V + 1, Y, X), F32),
            pltpu.VMEM(block, F32),
            pltpu.VMEM((16, PLANE), BF16),
            pltpu.VMEM((16, PLANE), BF16),
            pltpu.VMEM((16, PLANE), BF16),
            pltpu.VMEM((16, PLANE), BF16),
            pltpu.VMEM((2, 16, PLANE), BF16),
            pltpu.VMEM((2, 6, 8, PLANE), F32),
            pltpu.VMEM((2, ROWS, 8, PLANE), F32),
            pltpu.VMEM((2, ROWS, 8, PLANE), F32),
            dma,
            dma((CHUNKS,)),
            dma((CHUNKS,)),
            dma((CHUNKS,)),
            dma((CHUNKS,)),
            dma((2,)),
            dma((2,)),
            dma((2,)),
            dma((2,)),
        ],
        compiler_params=pltpu.CompilerParams(
            collective_id=0, has_side_effects=True, vmem_limit_bytes=32 << 20
        ),
        cost_estimate=pl.CostEstimate(flops=60_000_000, bytes_accessed=1_600_000, transcendentals=800_000),
    )(light_field)


def solution(mesh):
    return jax.shard_map(
        functools.partial(local, mesh.shape["views"], mesh.shape["cols"]),
        mesh=mesh,
        in_specs=(P("views", None, None, "cols"),),
        out_specs=P("views", None, None, "cols"),
        check_vma=False,
    )
```

```python
import functools

import jax
import jax.numpy as jnp
from jax import lax
from jax.experimental import pallas as pl
from jax.experimental.pallas import tpu as pltpu
from jax.sharding import PartitionSpec as P

MESH = pl.DeviceIdType.MESH
F32 = jnp.float32
BF16 = jnp.bfloat16
ROWS, V, Y, X = 2, 32, 32, 128
CHUNK = 2
CHUNKS = V // CHUNK
STEP = 4
H_CHUNK = 8
H_STEPS = V // H_CHUNK
FIRST = 2
SECOND = 9
EARLY = 3
PLANE = V * Y


def recip(x):
    r = pl.reciprocal(x, approx=True)
    return r * (2.0 - x * r)


def measures(first, cross, second):
    apart = second - first
    whole = second + first
    twice = cross + cross
    return apart * apart + twice * twice, whole * whole + 4096.0, cross, second + 64.0


def weighted(first, cross, second):
    spread, energy, cross, pivot = measures(first, cross, second)
    part = spread * recip(energy * pivot)
    return part * pivot + 0.1, part * cross


def join(weight_h, moment_h, first, cross, second):
    spread, energy, cross, pivot = measures(first, cross, second)
    above = moment_h * (energy * pivot) + spread * cross
    below = pivot * (energy * weight_h + spread)
    return -(above * recip(below))


def kernel(
    nv,
    nc,
    f_hbm,
    out,
    fv,
    full,
    got,
    wide,
    weight,
    moment,
    fix,
    slope,
    pack,
    pack_l,
    pack_r,
    mid,
    mids,
    edge,
    edge_j,
    edge_d,
    load_sem,
    near_s,
    near_r,
    far_s,
    far_r,
    pack_s,
    pack_rs,
    mid_s,
    mid_r,
):
    vi = lax.axis_index("views")
    cj = lax.axis_index("cols")
    odd = lax.rem(vi, 2)
    even = 1 - odd
    partner = vi + 1 - 2 * odd
    ahead = lax.rem(vi + nv + 2 - 4 * odd, nv)
    behind = lax.rem(vi + nv - 2 + 4 * odd, nv)
    left = lax.rem(cj + nc - 1, nc)
    right = lax.rem(cj + 1, nc)
    at_top = vi == 0
    at_bottom = vi == nv - 1
    has_far = jnp.logical_and(vi > 0, vi < nv - 1)
    sends_far = jnp.logical_and(vi != nv - 2, vi != 1)

    barrier = pltpu.get_barrier_semaphore()
    has_left, has_right = cj > 0, cj < nc - 1

    def greet(there):
        pl.semaphore_signal(barrier, inc=1, device_id=there, device_id_type=MESH)

    greet((partner, cj))
    for exists, there in ((has_far, (behind, cj)), (has_left, (vi, left)), (has_right, (vi, right))):

        @pl.when(exists)
        def _():
            greet(there)

    load = pltpu.make_async_copy(f_hbm, fv, load_sem)
    load.start()

    def remote(src, dst, s, r, there):
        return pltpu.make_async_remote_copy(
            src_ref=src, dst_ref=dst, send_sem=s, recv_sem=r, device_id=there, device_id_type=MESH
        )

    def near(k):
        span = pl.ds(k * CHUNK, CHUNK)
        return remote(f_hbm.at[:, span], got.at[odd, :, span], near_s.at[k], near_r.at[k], (partner, cj))

    def near_in(k):
        span = pl.ds(k * CHUNK, CHUNK)
        return remote(f_hbm.at[:, span], got.at[even, :, span], near_s.at[k], near_r.at[k], (partner, cj))

    def far(k):
        span = pl.ds(k * CHUNK, CHUNK)
        return remote(got.at[even, :, span], got.at[odd, :, span], far_s.at[k], far_r.at[k], (ahead, cj))

    to_left = remote(pack, pack_r, pack_s.at[0], pack_rs.at[0], (vi, left))
    to_right = remote(pack, pack_l, pack_s.at[1], pack_rs.at[1], (vi, right))

    one = jnp.int32(1)
    pl.semaphore_wait(
        barrier,
        one
        + jnp.where(sends_far, 1, 0)
        + jnp.where(has_left, 1, 0)
        + jnp.where(has_right, 1, 0),
    )
    for k in range(FIRST):
        near(k).start()
    load.wait()

    row8 = lax.broadcasted_iota(jnp.int32, (8, PLANE), 0)
    row16 = lax.broadcasted_iota(jnp.int32, (16, X), 0)
    lane16 = lax.broadcasted_iota(jnp.int32, (16, X), 1)
    r8 = lax.rem(row16, 8)
    wanted = jnp.where(r8 < 4, r8 + (X - 4), r8 - 4)

    packed = jnp.zeros((16, PLANE), F32)
    for u in range(ROWS):
        pick = jnp.where(jnp.logical_and(lane16 == wanted, row16 // 8 == u), 1.0, 0.0).astype(BF16)
        packed = packed + lax.dot_general(
            pick, fv[u].reshape(PLANE, X), (((1,), (1,)), ((), ())), preferred_element_type=F32
        )
    pack[...] = packed.astype(BF16)

    @pl.when(has_left)
    def _():
        to_left.start()

    @pl.when(has_right)
    def _():
        to_right.start()

    for k in range(FIRST, SECOND):
        near(k).start()

    @pl.when(at_top)
    def _():
        got[0, 0] = fv[0]
        got[0, 1] = jnp.zeros((V, Y, X), BF16)

    @pl.when(at_bottom)
    def _():
        got[1, 0] = jnp.zeros((V, Y, X), BF16)
        got[1, 1] = fv[1]

    def lanes(a, k):
        return pltpu.roll(a, (-k) % a.shape[-1], a.ndim - 1)

    def smooth_lanes(a):
        pair = a + lanes(a, -1)
        return pair + lanes(pair, 1)

    def horizontal(i, carry):
        before, last = carry
        u = i // H_STEPS
        v0 = lax.rem(i, H_STEPS) * H_CHUNK
        top = v0 == 0
        before = [jnp.where(top, 0.0, c) for c in before]
        last = [jnp.where(top, 0.0, c) for c in last]
        here = fv[u, pl.ds(v0, H_CHUNK)].astype(F32)
        full[u, pl.ds(v0, H_CHUNK)] = here
        above = jnp.where(top, 0.0, fv[u, jnp.maximum(v0 - 1, 0)].astype(F32))
        below = jnp.where(
            v0 + H_CHUNK < V, fv[u, jnp.minimum(v0 + H_CHUNK, V - 1)].astype(F32), 0.0
        )
        mid_x = jnp.concatenate([above[None], here, below[None]], 0)
        left_x, right_x = lanes(mid_x, -1), lanes(mid_x, 1)
        grad_v = [a[2:] - a[:-2] for a in (left_x, mid_x, right_x)]
        grad_x = [here - lanes(here, -2), right_x[1:-1] - left_x[1:-1], lanes(here, 2) - here]

        def smooth_x(p, q):
            a, b, c = (s * t for s, t in zip(p, q))
            return (a + c) + (b + b)

        now = [smooth_x(grad_v, grad_v), smooth_x(grad_v, grad_x), smooth_x(grad_x, grad_x)]
        run = [jnp.concatenate([a[None], b[None], c], 0) for a, b, c in zip(before, last, now)]
        pairs = [c[1:] + c[:-1] for c in run]
        w, m = weighted(*(c[1:] + c[:-1] for c in pairs))
        weight[u, pl.ds(v0, H_CHUNK)] = w
        moment[u, pl.ds(v0, H_CHUNK)] = m

        @pl.when(v0 == V - H_CHUNK)
        def _():
            w, m = weighted(*(c[-1] + d[-1] for c, d in zip(pairs, now)))
            weight[u, V] = w
            moment[u, V] = m

        return [c[H_CHUNK - 2] for c in now], [c[H_CHUNK - 1] for c in now]

    zeros = [jnp.zeros((Y, X), F32)] * 3
    lax.fori_loop(0, 2 * H_STEPS, horizontal, (zeros, zeros))

    def relay(k):
        near_in(k).wait_recv()

        @pl.when(sends_far)
        def _():
            far(k).start()

    for k in range(EARLY):
        relay(k)

    @pl.when(has_left)
    def _():
        to_right.wait_recv()

    @pl.when(has_right)
    def _():
        to_left.wait_recv()

    first, final = cj == 0, cj == nc - 1
    own = pack[...].astype(F32)
    from_l = pack_l[...].astype(F32)
    from_r = pack_r[...].astype(F32)
    mixed = []
    for u in range(ROWS):
        mine = own[8 * u : 8 * u + 8]
        l_in = from_l[8 * u : 8 * u + 8]
        r_in = from_r[8 * u : 8 * u + 8]
        flip_l = jnp.where(row8 == 2, pltpu.roll(mine, 6, 0), 0.0)
        flip_r = jnp.where(row8 == 5, pltpu.roll(mine, 2, 0), 0.0)
        l_in = jnp.where(first, flip_l, l_in)
        r_in = jnp.where(final, flip_r, r_in)
        e_l = jnp.where(row8 < 4, l_in, mine)
        e_r = jnp.where(row8 < 4, mine, r_in)
        edge[0, 2 + u] = e_l
        edge[1, 2 + u] = e_r
        mixed.append(jnp.where(jnp.logical_and(row8 >= 2, row8 < 6), e_l, pltpu.roll(e_r, 4, 0)))
    mid[...] = jnp.concatenate(mixed, axis=0).astype(BF16)
    mid_near = remote(mid, mids.at[odd], mid_s.at[0], mid_r.at[0], (partner, cj))
    mid_near_in = remote(mid, mids.at[even], mid_s.at[0], mid_r.at[0], (partner, cj))
    mid_far = remote(mids.at[even], mids.at[odd], mid_s.at[1], mid_r.at[1], (ahead, cj))
    mid_near.start()
    for k in range(SECOND, CHUNKS):
        near(k).start()

    lane = lax.broadcasted_iota(jnp.int32, (STEP, 8, X), 2)
    sub = lax.broadcasted_iota(jnp.int32, (STEP, 8, X), 1)
    rim = jnp.logical_or(lane < 2, lane >= X - 2)
    outer = jnp.logical_or(lane == 0, lane == X - 1)

    def parts(ref, *at):
        return [ref[(*at, pl.ds(p, 8, stride=4), slice(None))] for p in range(4)]

    def y_up(a, rest=0.0):
        return a[1:] + [jnp.where(sub == 7, rest, pltpu.roll(a[0], 7, 1))]

    def y_down(a):
        return [jnp.where(sub == 0, 0.0, pltpu.roll(a[3], 1, 1))] + a[:3]

    def smooth_y(a):
        pair = [b + c for b, c in zip(a, y_down(a))]
        return [b + c for b, c in zip(pair, y_up(pair, a[3]))]

    def vertical(v0):
        span = pl.ds(v0, STEP)
        for slot in range(2):
            for u in range(ROWS):
                wide[2 * slot + u] = got[slot, u, span].astype(F32)
        every = slice(None)
        field = (
            [parts(wide, 0, every), parts(wide, 1, every)]
            + [parts(full, u, span) for u in range(ROWS)]
            + [parts(wide, 2, every), parts(wide, 3, every)]
        )
        comps = []
        for r in range(1, 5):
            grad_u = [a - b for a, b in zip(field[r + 1], field[r - 1])]
            grad_y = [a - b for a, b in zip(y_up(field[r]), y_down(field[r]))]
            comps.append(
                [
                    [a * b for a, b in zip(g, h)]
                    for g, h in ((grad_u, grad_u), (grad_u, grad_y), (grad_y, grad_y))
                ]
            )
        pairs = [
            [[a + b for a, b in zip(c, d)] for c, d in zip(comps[r], comps[r + 1])] for r in range(3)
        ]
        for u in range(ROWS):
            tensor = [
                smooth_y([a + b for a, b in zip(c, d)]) for c, d in zip(pairs[u], pairs[u + 1])
            ]
            past = pl.ds(v0 + 1, STEP)
            w, m = parts(weight, u, past), parts(moment, u, past)
            for p in range(4):
                slope[u, span, p] = join(w[p], m[p], *(c[p] for c in tensor))

    def variation(v0):
        span = pl.ds(v0, STEP)
        for u in range(ROWS):
            t = parts(fix, u, span)
            joined = [jnp.where(rim, t[p], slope[u, span, p]) for p in range(4)]
            flux_x, flux_y = [], []
            for here, below in zip(joined, y_up(joined)):
                step_x = lanes(here, 1) - here
                step_y = below - here
                scale = lax.rsqrt(step_x * step_x + step_y * step_y + 1.0)
                flux_x.append(step_x * scale)
                flux_y.append(step_y * scale)
            for p, above in enumerate(y_down(flux_y)):
                depth = joined[p] + 0.2 * (flux_x[p] - lanes(flux_x[p], -1) + flux_y[p] - above)
                out[u, span, pl.ds(p, 8, stride=4), :] = jnp.where(outer, lanes(t[p], -63), depth)

    for k in range(EARLY, EARLY + 2):
        relay(k)

    def arrived(g):
        @pl.when(has_far)
        def _():
            far(2 * g).wait_recv()
            far(2 * g + 1).wait_recv()

    def start(g, carry):
        relay(2 * g + EARLY + 2)
        relay(2 * g + EARLY + 3)

        @pl.when(g == 1)
        def _():
            mid_near_in.wait_recv()

            @pl.when(sends_far)
            def _():
                mid_far.start()

        arrived(g)
        vertical(g * STEP)
        return carry

    lax.fori_loop(0, 4, start, 0)

    @pl.when(has_far)
    def _():
        mid_far.wait_recv()

    for slot in range(2):
        rows_in = mids[slot].astype(F32)
        for u in range(ROWS):
            tile = rows_in[8 * u : 8 * u + 8]
            edge[0, 4 * slot + u] = tile
            edge[1, 4 * slot + u] = pltpu.roll(tile, 4, 0)

    @pl.when(at_top)
    def _():
        for side in range(2):
            edge[side, 0] = edge[side, 2]
            edge[side, 1] = jnp.zeros((8, PLANE), F32)

    @pl.when(at_bottom)
    def _():
        for side in range(2):
            edge[side, 4] = jnp.zeros((8, PLANE), F32)
            edge[side, 5] = edge[side, 3]

    place = lax.broadcasted_iota(jnp.int32, (8, PLANE), 1)
    y_at = lax.rem(place, Y)

    def cols_by(a, k):
        return pltpu.roll(a, (-k) % 8, 0)

    def y_by(a, k):
        return jnp.where(y_at == (Y - 1 if k > 0 else 0), 0.0, pltpu.roll(a, (-k) % PLANE, 1))

    def v_by(a, k):
        return jnp.where(
            place >= PLANE - Y if k > 0 else place < Y, 0.0, pltpu.roll(a, (-k * Y) % PLANE, 1)
        )

    def smooth_by(by, a):
        return by(a, -1) + (a + a) + by(a, 1)

    def edges(side, carry):
        j_below = jnp.where(jnp.logical_and(final, side == 1), 4, 8)
        q_from = jnp.where(jnp.logical_and(first, side == 0), 4, 0)
        tiles = [edge[side, r] for r in range(6)]
        comps = []
        for r in range(1, 5):
            grad_u = tiles[r + 1] - tiles[r - 1]
            grad_y = y_by(tiles[r], 1) - y_by(tiles[r], -1)
            comps.append((grad_u * grad_u, grad_u * grad_y, grad_y * grad_y))
        for u in range(ROWS):
            f = tiles[2 + u]
            grad_v = v_by(f, 1) - v_by(f, -1)
            grad_x = cols_by(f, 1) - cols_by(f, -1)
            w, m = weighted(
                *(
                    smooth_by(v_by, smooth_by(cols_by, c))
                    for c in (grad_v * grad_v, grad_v * grad_x, grad_x * grad_x)
                )
            )
            tensor = [
                smooth_by(y_by, a + (b + b) + c) for a, b, c in zip(comps[u], comps[u + 1], comps[u + 2])
            ]
            joined = jnp.where(row8 < j_below, join(w, m, *tensor), 0.0)
            step_x = cols_by(joined, 1) - joined
            step_y = y_by(joined, 1) - joined
            scale = lax.rsqrt(step_x * step_x + step_y * step_y + 1.0)
            flux_x = jnp.where(row8 >= q_from, step_x * scale, 0.0)
            flux_y = step_y * scale
            depth = joined + 0.2 * (flux_x - cols_by(flux_x, -1) + flux_y - y_by(flux_y, -1))
            edge_j[side, u] = pltpu.roll(joined, 4, 0)
            edge_d[side, u] = pltpu.roll(depth, 5, 0)
        relay(EARLY + 10 + side)
        return carry

    lax.fori_loop(0, 2, edges, 0)

    small = lax.broadcasted_iota(jnp.int32, (8, X), 0)

    def spread_out(u, carry):
        for b in range(PLANE // X):
            part = pl.ds(b * X, X)
            both = jnp.where(small == 0, edge_d[1, u, :, part], edge_d[0, u, :, part])
            block = jnp.concatenate(
                [
                    edge_j[0, u, :, part],
                    jnp.zeros((56, X), F32),
                    both,
                    jnp.zeros((48, X), F32),
                    edge_j[1, u, :, part],
                ],
                axis=0,
            )
            fix[u, pl.ds(4 * b, 4)] = block.T.reshape(4, Y, X)
        return carry

    lax.fori_loop(0, 2, spread_out, 0)

    for k in range(EARLY + 12, CHUNKS):
        relay(k)

    def finish(i, carry):
        arrived(4 + i)
        vertical((4 + i) * STEP)
        variation(2 * i * STEP)
        variation((2 * i + 1) * STEP)
        return carry

    lax.fori_loop(0, 4, finish, 0)

    @pl.when(has_left)
    def _():
        to_left.wait_send()

    @pl.when(has_right)
    def _():
        to_right.wait_send()

    mid_near.wait_send()
    for k in range(CHUNKS):
        near(k).wait_send()

    @pl.when(sends_far)
    def _():
        mid_far.wait_send()
        for k in range(CHUNKS):
            far(k).wait_send()


def local(nv, nc, light_field):
    block = (ROWS, V, Y, X)
    dma = pltpu.SemaphoreType.DMA
    return pl.pallas_call(
        functools.partial(kernel, nv, nc),
        out_shape=jax.ShapeDtypeStruct(block, F32),
        in_specs=[pl.BlockSpec(memory_space=pl.ANY)],
        out_specs=pl.BlockSpec(memory_space=pltpu.VMEM),
        scratch_shapes=[
            pltpu.VMEM(block, BF16),
            pltpu.VMEM(block, F32),
            pltpu.VMEM((2, *block), BF16),
            pltpu.VMEM((4, STEP, Y, X), F32),
            pltpu.VMEM((ROWS, V + 1, Y, X), F32),
            pltpu.VMEM((ROWS, V + 1, Y, X), F32),
            pltpu.VMEM(block, F32),
            pltpu.VMEM((ROWS, V, 4, 8, X), F32),
            pltpu.VMEM((16, PLANE), BF16),
            pltpu.VMEM((16, PLANE), BF16),
            pltpu.VMEM((16, PLANE), BF16),
            pltpu.VMEM((16, PLANE), BF16),
            pltpu.VMEM((2, 16, PLANE), BF16),
            pltpu.VMEM((2, 6, 8, PLANE), F32),
            pltpu.VMEM((2, ROWS, 8, PLANE), F32),
            pltpu.VMEM((2, ROWS, 8, PLANE), F32),
            dma,
            dma((CHUNKS,)),
            dma((CHUNKS,)),
            dma((CHUNKS,)),
            dma((CHUNKS,)),
            dma((2,)),
            dma((2,)),
            dma((2,)),
            dma((2,)),
        ],
        compiler_params=pltpu.CompilerParams(
            collective_id=0, has_side_effects=True, vmem_limit_bytes=32 << 20
        ),
        cost_estimate=pl.CostEstimate(flops=60_000_000, bytes_accessed=1_600_000, transcendentals=800_000),
    )(pltpu.with_memory_space_constraint(light_field, pltpu.HBM))


def solution(mesh):
    return jax.shard_map(
        functools.partial(local, mesh.shape["views"], mesh.shape["cols"]),
        mesh=mesh,
        in_specs=(P("views", None, None, "cols"),),
        out_specs=P("views", None, None, "cols"),
        check_vma=False,
    )
```

```python
import functools

import jax
import jax.numpy as jnp
from jax import lax
from jax.experimental import pallas as pl
from jax.experimental.pallas import tpu as pltpu
from jax.sharding import PartitionSpec as P

MESH = pl.DeviceIdType.MESH
F32 = jnp.float32
BF16 = jnp.bfloat16
ROWS, V, Y, X = 2, 32, 32, 128
CHUNK = 2
CHUNKS = V // CHUNK
STEP = 4
H_CHUNK = 8
H_STEPS = V // H_CHUNK
FIRST = 6
PLANE = V * Y


def recip(x):
    r = pl.reciprocal(x, approx=True)
    return r * (2.0 - x * r)


def measures(first, cross, second):
    apart = second - first
    whole = second + first
    twice = cross + cross
    return apart * apart + twice * twice, whole * whole + 4096.0, cross, second + 64.0


def weighted(first, cross, second):
    spread, energy, cross, pivot = measures(first, cross, second)
    part = spread * recip(energy * pivot)
    return part * pivot + 0.1, part * cross


def join(weight_h, moment_h, first, cross, second):
    spread, energy, cross, pivot = measures(first, cross, second)
    above = moment_h * (energy * pivot) + spread * cross
    below = pivot * (energy * weight_h + spread)
    return -(above * recip(below))


def kernel(
    nv,
    nc,
    f_hbm,
    out,
    fv,
    full,
    got,
    wide,
    weight,
    moment,
    fix,
    slope,
    pack,
    pack_l,
    pack_r,
    mid,
    mids,
    edge,
    edge_j,
    edge_d,
    load_sem,
    near_s,
    near_r,
    far_s,
    far_r,
    pack_s,
    pack_rs,
    mid_s,
    mid_r,
):
    vi = lax.axis_index("views")
    cj = lax.axis_index("cols")
    odd = lax.rem(vi, 2)
    even = 1 - odd
    partner = vi + 1 - 2 * odd
    ahead = lax.rem(vi + nv + 2 - 4 * odd, nv)
    behind = lax.rem(vi + nv - 2 + 4 * odd, nv)
    left = lax.rem(cj + nc - 1, nc)
    right = lax.rem(cj + 1, nc)
    at_top = vi == 0
    at_bottom = vi == nv - 1
    has_far = jnp.logical_and(vi > 0, vi < nv - 1)
    sends_far = jnp.logical_and(vi != nv - 2, vi != 1)

    barrier = pltpu.get_barrier_semaphore()
    has_left, has_right = cj > 0, cj < nc - 1

    def greet(there):
        pl.semaphore_signal(barrier, inc=1, device_id=there, device_id_type=MESH)

    greet((partner, cj))
    for exists, there in ((has_far, (behind, cj)), (has_left, (vi, left)), (has_right, (vi, right))):

        @pl.when(exists)
        def _():
            greet(there)

    load = pltpu.make_async_copy(f_hbm, fv, load_sem)
    load.start()

    def remote(src, dst, s, r, there):
        return pltpu.make_async_remote_copy(
            src_ref=src, dst_ref=dst, send_sem=s, recv_sem=r, device_id=there, device_id_type=MESH
        )

    def near(k):
        span = pl.ds(k * CHUNK, CHUNK)
        return remote(f_hbm.at[:, span], got.at[odd, :, span], near_s.at[k], near_r.at[k], (partner, cj))

    def near_in(k):
        span = pl.ds(k * CHUNK, CHUNK)
        return remote(f_hbm.at[:, span], got.at[even, :, span], near_s.at[k], near_r.at[k], (partner, cj))

    def far(k):
        span = pl.ds(k * CHUNK, CHUNK)
        return remote(got.at[even, :, span], got.at[odd, :, span], far_s.at[k], far_r.at[k], (ahead, cj))

    to_left = remote(pack, pack_r, pack_s.at[0], pack_rs.at[0], (vi, left))
    to_right = remote(pack, pack_l, pack_s.at[1], pack_rs.at[1], (vi, right))

    load.wait()

    row8 = lax.broadcasted_iota(jnp.int32, (8, PLANE), 0)
    row16 = lax.broadcasted_iota(jnp.int32, (16, X), 0)
    lane16 = lax.broadcasted_iota(jnp.int32, (16, X), 1)
    r8 = lax.rem(row16, 8)
    wanted = jnp.where(r8 < 4, r8 + (X - 4), r8 - 4)

    packed = jnp.zeros((16, PLANE), F32)
    for u in range(ROWS):
        pick = jnp.where(jnp.logical_and(lane16 == wanted, row16 // 8 == u), 1.0, 0.0).astype(BF16)
        packed = packed + lax.dot_general(
            pick, fv[u].reshape(PLANE, X), (((1,), (1,)), ((), ())), preferred_element_type=F32
        )
    pack[...] = packed.astype(BF16)

    one = jnp.int32(1)
    pl.semaphore_wait(
        barrier,
        one
        + jnp.where(sends_far, 1, 0)
        + jnp.where(has_left, 1, 0)
        + jnp.where(has_right, 1, 0),
    )
    @pl.when(has_left)
    def _():
        to_left.start()

    @pl.when(has_right)
    def _():
        to_right.start()

    for k in range(FIRST):
        near(k).start()

    @pl.when(at_top)
    def _():
        got[0, 0] = fv[0]
        got[0, 1] = jnp.zeros((V, Y, X), BF16)

    @pl.when(at_bottom)
    def _():
        got[1, 0] = jnp.zeros((V, Y, X), BF16)
        got[1, 1] = fv[1]

    def lanes(a, k):
        return pltpu.roll(a, (-k) % a.shape[-1], a.ndim - 1)

    def smooth_lanes(a):
        pair = a + lanes(a, -1)
        return pair + lanes(pair, 1)

    def horizontal(i, carry):
        before, last = carry
        u = i // H_STEPS
        v0 = lax.rem(i, H_STEPS) * H_CHUNK
        top = v0 == 0
        before = [jnp.where(top, 0.0, c) for c in before]
        last = [jnp.where(top, 0.0, c) for c in last]
        here = fv[u, pl.ds(v0, H_CHUNK)].astype(F32)
        full[u, pl.ds(v0, H_CHUNK)] = here
        above = jnp.where(top, 0.0, fv[u, jnp.maximum(v0 - 1, 0)].astype(F32))
        below = jnp.where(
            v0 + H_CHUNK < V, fv[u, jnp.minimum(v0 + H_CHUNK, V - 1)].astype(F32), 0.0
        )
        mid_x = jnp.concatenate([above[None], here, below[None]], 0)
        left_x, right_x = lanes(mid_x, -1), lanes(mid_x, 1)
        grad_v = [a[2:] - a[:-2] for a in (left_x, mid_x, right_x)]
        grad_x = [here - lanes(here, -2), right_x[1:-1] - left_x[1:-1], lanes(here, 2) - here]

        def smooth_x(p, q):
            a, b, c = (s * t for s, t in zip(p, q))
            return (a + c) + (b + b)

        now = [smooth_x(grad_v, grad_v), smooth_x(grad_v, grad_x), smooth_x(grad_x, grad_x)]
        run = [jnp.concatenate([a[None], b[None], c], 0) for a, b, c in zip(before, last, now)]
        pairs = [c[1:] + c[:-1] for c in run]
        w, m = weighted(*(c[1:] + c[:-1] for c in pairs))
        weight[u, pl.ds(v0, H_CHUNK)] = w
        moment[u, pl.ds(v0, H_CHUNK)] = m

        @pl.when(v0 == V - H_CHUNK)
        def _():
            w, m = weighted(*(c[-1] + d[-1] for c, d in zip(pairs, now)))
            weight[u, V] = w
            moment[u, V] = m

        return [c[H_CHUNK - 2] for c in now], [c[H_CHUNK - 1] for c in now]

    zeros = [jnp.zeros((Y, X), F32)] * 3
    lax.fori_loop(0, 2 * H_STEPS, horizontal, (zeros, zeros))

    @pl.when(has_left)
    def _():
        to_right.wait_recv()

    @pl.when(has_right)
    def _():
        to_left.wait_recv()

    first, final = cj == 0, cj == nc - 1
    own = pack[...].astype(F32)
    from_l = pack_l[...].astype(F32)
    from_r = pack_r[...].astype(F32)
    mixed = []
    for u in range(ROWS):
        mine = own[8 * u : 8 * u + 8]
        l_in = from_l[8 * u : 8 * u + 8]
        r_in = from_r[8 * u : 8 * u + 8]
        flip_l = jnp.where(row8 == 2, pltpu.roll(mine, 6, 0), 0.0)
        flip_r = jnp.where(row8 == 5, pltpu.roll(mine, 2, 0), 0.0)
        l_in = jnp.where(first, flip_l, l_in)
        r_in = jnp.where(final, flip_r, r_in)
        e_l = jnp.where(row8 < 4, l_in, mine)
        e_r = jnp.where(row8 < 4, mine, r_in)
        edge[0, 2 + u] = e_l
        edge[1, 2 + u] = e_r
        mixed.append(jnp.where(jnp.logical_and(row8 >= 2, row8 < 6), e_l, pltpu.roll(e_r, 4, 0)))
    mid[...] = jnp.concatenate(mixed, axis=0).astype(BF16)
    mid_near = remote(mid, mids.at[odd], mid_s.at[0], mid_r.at[0], (partner, cj))
    mid_near_in = remote(mid, mids.at[even], mid_s.at[0], mid_r.at[0], (partner, cj))
    mid_far = remote(mids.at[even], mids.at[odd], mid_s.at[1], mid_r.at[1], (ahead, cj))
    mid_near.start()
    for k in range(FIRST, CHUNKS):
        near(k).start()

    def relay(k):
        near_in(k).wait_recv()

        @pl.when(sends_far)
        def _():
            far(k).start()

    relay(0)

    lane = lax.broadcasted_iota(jnp.int32, (STEP, 8, X), 2)
    sub = lax.broadcasted_iota(jnp.int32, (STEP, 8, X), 1)
    rim = jnp.logical_or(lane < 2, lane >= X - 2)
    outer = jnp.logical_or(lane == 0, lane == X - 1)

    def parts(ref, *at):
        return [ref[(*at, pl.ds(p, 8, stride=4), slice(None))] for p in range(4)]

    def y_up(a, rest=0.0):
        return a[1:] + [jnp.where(sub == 7, rest, pltpu.roll(a[0], 7, 1))]

    def y_down(a):
        return [jnp.where(sub == 0, 0.0, pltpu.roll(a[3], 1, 1))] + a[:3]

    def smooth_y(a):
        pair = [b + c for b, c in zip(a, y_down(a))]
        return [b + c for b, c in zip(pair, y_up(pair, a[3]))]

    def vertical(v0):
        span = pl.ds(v0, STEP)
        for slot in range(2):
            for u in range(ROWS):
                wide[2 * slot + u] = got[slot, u, span].astype(F32)
        every = slice(None)
        field = (
            [parts(wide, 0, every), parts(wide, 1, every)]
            + [parts(full, u, span) for u in range(ROWS)]
            + [parts(wide, 2, every), parts(wide, 3, every)]
        )
        comps = []
        for r in range(1, 5):
            grad_u = [a - b for a, b in zip(field[r + 1], field[r - 1])]
            grad_y = [a - b for a, b in zip(y_up(field[r]), y_down(field[r]))]
            comps.append(
                [
                    [a * b for a, b in zip(g, h)]
                    for g, h in ((grad_u, grad_u), (grad_u, grad_y), (grad_y, grad_y))
                ]
            )
        pairs = [
            [[a + b for a, b in zip(c, d)] for c, d in zip(comps[r], comps[r + 1])] for r in range(3)
        ]
        for u in range(ROWS):
            tensor = [
                smooth_y([a + b for a, b in zip(c, d)]) for c, d in zip(pairs[u], pairs[u + 1])
            ]
            past = pl.ds(v0 + 1, STEP)
            w, m = parts(weight, u, past), parts(moment, u, past)
            for p in range(4):
                slope[u, span, p] = join(w[p], m[p], *(c[p] for c in tensor))

    def variation(v0):
        span = pl.ds(v0, STEP)
        for u in range(ROWS):
            t = parts(fix, u, span)
            joined = [jnp.where(rim, t[p], slope[u, span, p]) for p in range(4)]
            flux_x, flux_y = [], []
            for here, below in zip(joined, y_up(joined)):
                step_x = lanes(here, 1) - here
                step_y = below - here
                scale = lax.rsqrt(step_x * step_x + step_y * step_y + 1.0)
                flux_x.append(step_x * scale)
                flux_y.append(step_y * scale)
            for p, above in enumerate(y_down(flux_y)):
                depth = joined[p] + 0.2 * (flux_x[p] - lanes(flux_x[p], -1) + flux_y[p] - above)
                out[u, span, pl.ds(p, 8, stride=4), :] = jnp.where(outer, lanes(t[p], -63), depth)

    place = lax.broadcasted_iota(jnp.int32, (8, PLANE), 1)
    y_at = lax.rem(place, Y)

    def cols_by(a, k):
        return pltpu.roll(a, (-k) % 8, 0)

    def y_by(a, k):
        return jnp.where(y_at == (Y - 1 if k > 0 else 0), 0.0, pltpu.roll(a, (-k) % PLANE, 1))

    def v_by(a, k):
        return jnp.where(
            place >= PLANE - Y if k > 0 else place < Y, 0.0, pltpu.roll(a, (-k * Y) % PLANE, 1)
        )

    def smooth_by(by, a):
        return by(a, -1) + (a + a) + by(a, 1)

    def edges_h(side, carry):
        for u in range(ROWS):
            f = edge[side, 2 + u]
            grad_v = v_by(f, 1) - v_by(f, -1)
            grad_x = cols_by(f, 1) - cols_by(f, -1)
            w, m = weighted(
                *(
                    smooth_by(v_by, smooth_by(cols_by, c))
                    for c in (grad_v * grad_v, grad_v * grad_x, grad_x * grad_x)
                )
            )
            edge_j[side, u] = w
            edge_d[side, u] = m
        return carry

    lax.fori_loop(0, 2, edges_h, 0)
    for k in range(1, 6):
        relay(k)
    mid_near_in.wait_recv()

    @pl.when(sends_far)
    def _():
        mid_far.start()

    def arrived(g):
        @pl.when(has_far)
        def _():
            far(2 * g).wait_recv()
            far(2 * g + 1).wait_recv()

    def start(g, carry):
        relay(2 * g + 6)
        relay(2 * g + 7)
        arrived(g)
        vertical(g * STEP)
        return carry

    lax.fori_loop(0, 2, start, 0)

    @pl.when(has_far)
    def _():
        mid_far.wait_recv()

    for slot in range(2):
        rows_in = mids[slot].astype(F32)
        for u in range(ROWS):
            tile = rows_in[8 * u : 8 * u + 8]
            edge[0, 4 * slot + u] = tile
            edge[1, 4 * slot + u] = pltpu.roll(tile, 4, 0)

    @pl.when(at_top)
    def _():
        for side in range(2):
            edge[side, 0] = edge[side, 2]
            edge[side, 1] = jnp.zeros((8, PLANE), F32)

    @pl.when(at_bottom)
    def _():
        for side in range(2):
            edge[side, 4] = jnp.zeros((8, PLANE), F32)
            edge[side, 5] = edge[side, 3]

    def edges(side, carry):
        j_below = jnp.where(jnp.logical_and(final, side == 1), 4, 8)
        q_from = jnp.where(jnp.logical_and(first, side == 0), 4, 0)
        tiles = [edge[side, r] for r in range(6)]
        comps = []
        for r in range(1, 5):
            grad_u = tiles[r + 1] - tiles[r - 1]
            grad_y = y_by(tiles[r], 1) - y_by(tiles[r], -1)
            comps.append((grad_u * grad_u, grad_u * grad_y, grad_y * grad_y))
        for u in range(ROWS):
            w, m = edge_j[side, u], edge_d[side, u]
            tensor = [
                smooth_by(y_by, a + (b + b) + c) for a, b, c in zip(comps[u], comps[u + 1], comps[u + 2])
            ]
            joined = jnp.where(row8 < j_below, join(w, m, *tensor), 0.0)
            step_x = cols_by(joined, 1) - joined
            step_y = y_by(joined, 1) - joined
            scale = lax.rsqrt(step_x * step_x + step_y * step_y + 1.0)
            flux_x = jnp.where(row8 >= q_from, step_x * scale, 0.0)
            flux_y = step_y * scale
            depth = joined + 0.2 * (flux_x - cols_by(flux_x, -1) + flux_y - y_by(flux_y, -1))
            edge_j[side, u] = pltpu.roll(joined, 4, 0)
            edge_d[side, u] = pltpu.roll(depth, 5, 0)
        relay(10 + side)
        return carry

    lax.fori_loop(0, 2, edges, 0)

    small = lax.broadcasted_iota(jnp.int32, (8, X), 0)

    def spread_out(u, carry):
        for b in range(PLANE // X):
            part = pl.ds(b * X, X)
            both = jnp.where(small == 0, edge_d[1, u, :, part], edge_d[0, u, :, part])
            block = jnp.concatenate(
                [
                    edge_j[0, u, :, part],
                    jnp.zeros((56, X), F32),
                    both,
                    jnp.zeros((48, X), F32),
                    edge_j[1, u, :, part],
                ],
                axis=0,
            )
            fix[u, pl.ds(4 * b, 4)] = block.T.reshape(4, Y, X)
        return carry

    lax.fori_loop(0, 2, spread_out, 0)

    def finish(g, carry):
        for k in range(2):

            @pl.when(2 * g + k + 8 < CHUNKS)
            def _():
                relay(2 * g + k + 8)

        def varied(i, c):
            variation(i * STEP)
            return c

        lax.fori_loop(jnp.where(g < 4, g - 2, g - 1), jnp.where(g == 2, 1, g), varied, 0)
        arrived(g)
        vertical(g * STEP)
        return carry

    lax.fori_loop(2, V // STEP, finish, 0)
    variation(V - STEP)

    @pl.when(has_left)
    def _():
        to_left.wait_send()

    @pl.when(has_right)
    def _():
        to_right.wait_send()

    mid_near.wait_send()
    for k in range(CHUNKS):
        near(k).wait_send()

    @pl.when(sends_far)
    def _():
        mid_far.wait_send()
        for k in range(CHUNKS):
            far(k).wait_send()


def local(nv, nc, light_field):
    block = (ROWS, V, Y, X)
    dma = pltpu.SemaphoreType.DMA
    return pl.pallas_call(
        functools.partial(kernel, nv, nc),
        out_shape=jax.ShapeDtypeStruct(block, F32),
        in_specs=[pl.BlockSpec(memory_space=pl.ANY)],
        out_specs=pl.BlockSpec(memory_space=pltpu.VMEM),
        scratch_shapes=[
            pltpu.VMEM(block, BF16),
            pltpu.VMEM(block, F32),
            pltpu.VMEM((2, *block), BF16),
            pltpu.VMEM((4, STEP, Y, X), F32),
            pltpu.VMEM((ROWS, V + 1, Y, X), F32),
            pltpu.VMEM((ROWS, V + 1, Y, X), F32),
            pltpu.VMEM(block, F32),
            pltpu.VMEM((ROWS, V, 4, 8, X), F32),
            pltpu.VMEM((16, PLANE), BF16),
            pltpu.VMEM((16, PLANE), BF16),
            pltpu.VMEM((16, PLANE), BF16),
            pltpu.VMEM((16, PLANE), BF16),
            pltpu.VMEM((2, 16, PLANE), BF16),
            pltpu.VMEM((2, 6, 8, PLANE), F32),
            pltpu.VMEM((2, ROWS, 8, PLANE), F32),
            pltpu.VMEM((2, ROWS, 8, PLANE), F32),
            dma,
            dma((CHUNKS,)),
            dma((CHUNKS,)),
            dma((CHUNKS,)),
            dma((CHUNKS,)),
            dma((2,)),
            dma((2,)),
            dma((2,)),
            dma((2,)),
        ],
        compiler_params=pltpu.CompilerParams(
            collective_id=0, has_side_effects=True, vmem_limit_bytes=32 << 20
        ),
        cost_estimate=pl.CostEstimate(flops=60_000_000, bytes_accessed=1_600_000, transcendentals=800_000),
    )(pltpu.with_memory_space_constraint(light_field, pltpu.HBM))


def solution(mesh):
    return jax.shard_map(
        functools.partial(local, mesh.shape["views"], mesh.shape["cols"]),
        mesh=mesh,
        in_specs=(P("views", None, None, "cols"),),
        out_specs=P("views", None, None, "cols"),
        check_vma=False,
    )
```

```python
import functools

import jax
import jax.numpy as jnp
from jax import lax
from jax.experimental import pallas as pl
from jax.experimental.pallas import tpu as pltpu
from jax.sharding import PartitionSpec as P

MESH = pl.DeviceIdType.MESH
F32 = jnp.float32
BF16 = jnp.bfloat16
ROWS, V, Y, X = 2, 32, 32, 128
CHUNK = 2
CHUNKS = V // CHUNK
STEP = 4
H_CHUNK = 8
H_STEPS = V // H_CHUNK
BEFORE = 3
FIRST = 6
FLIGHT = 8
PLANE = V * Y


def recip(x):
    r = pl.reciprocal(x, approx=True)
    return r * (2.0 - x * r)


def measures(first, cross, second):
    apart = second - first
    whole = second + first
    twice = cross + cross
    return apart * apart + twice * twice, whole * whole + 4096.0, cross, second + 64.0


def weighted(first, cross, second):
    spread, energy, cross, pivot = measures(first, cross, second)
    part = spread * recip(energy * pivot)
    return part * pivot + 0.1, part * cross


def join(weight_h, moment_h, first, cross, second):
    spread, energy, cross, pivot = measures(first, cross, second)
    above = moment_h * (energy * pivot) + spread * cross
    below = pivot * (energy * weight_h + spread)
    return -(above * recip(below))


def kernel(
    nv,
    nc,
    f_hbm,
    out,
    fv,
    full,
    got,
    wide,
    weight,
    moment,
    fix,
    slope,
    pack,
    pack_out,
    pack_l,
    pack_r,
    own_cols,
    cols_in,
    edge,
    edge_j,
    edge_d,
    load_sem,
    near_s,
    near_r,
    far_s,
    far_r,
    pack_s,
    pack_rs,
    cols_s,
    cols_r,
):
    vi = lax.axis_index("views")
    cj = lax.axis_index("cols")
    odd = lax.rem(vi, 2)
    even = 1 - odd
    partner = vi + 1 - 2 * odd
    ahead = lax.rem(vi + nv + 2 - 4 * odd, nv)
    behind = lax.rem(vi + nv - 2 + 4 * odd, nv)
    left = lax.rem(cj + nc - 1, nc)
    right = lax.rem(cj + 1, nc)
    at_top = vi == 0
    at_bottom = vi == nv - 1
    has_far = jnp.logical_and(vi > 0, vi < nv - 1)
    sends_far = jnp.logical_and(vi != nv - 2, vi != 1)

    barrier = pltpu.get_barrier_semaphore()
    has_left, has_right = cj > 0, cj < nc - 1

    def greet(there):
        pl.semaphore_signal(barrier, inc=1, device_id=there, device_id_type=MESH)

    greet((partner, cj))
    for exists, there in ((has_far, (behind, cj)), (has_left, (vi, left)), (has_right, (vi, right))):

        @pl.when(exists)
        def _():
            greet(there)

    load = pltpu.make_async_copy(f_hbm, fv, load_sem)
    load.start()

    def remote(src, dst, s, r, there):
        return pltpu.make_async_remote_copy(
            src_ref=src, dst_ref=dst, send_sem=s, recv_sem=r, device_id=there, device_id_type=MESH
        )

    def near(k):
        span = pl.ds(k * CHUNK, CHUNK)
        return remote(f_hbm.at[:, span], got.at[odd, :, span], near_s, near_r.at[k], (partner, cj))

    def near_in(k):
        span = pl.ds(k * CHUNK, CHUNK)
        return remote(f_hbm.at[:, span], got.at[even, :, span], near_s, near_r.at[k], (partner, cj))

    def far(k):
        span = pl.ds(k * CHUNK, CHUNK)
        return remote(got.at[even, :, span], got.at[odd, :, span], far_s, far_r.at[k // 2], (ahead, cj))

    to_left = remote(pack_out.at[0], pack_r, pack_s.at[0], pack_rs.at[0], (vi, left))
    to_right = remote(pack_out.at[1], pack_l, pack_s.at[1], pack_rs.at[1], (vi, right))

    load.wait()

    row8 = lax.broadcasted_iota(jnp.int32, (8, PLANE), 0)
    row16 = lax.broadcasted_iota(jnp.int32, (16, X), 0)
    lane16 = lax.broadcasted_iota(jnp.int32, (16, X), 1)
    r8 = lax.rem(row16, 8)
    wanted = jnp.where(r8 < 4, r8 + (X - 4), r8 - 4)

    packed = jnp.zeros((16, PLANE), F32)
    for u in range(ROWS):
        pick = jnp.where(jnp.logical_and(lane16 == wanted, row16 // 8 == u), 1.0, 0.0).astype(BF16)
        packed = packed + lax.dot_general(
            pick, fv[u].reshape(PLANE, X), (((1,), (1,)), ((), ())), preferred_element_type=F32
        )
    pack[...] = packed.astype(BF16)

    def folded(a):
        return jnp.concatenate([a[:, : PLANE // 2], a[:, PLANE // 2 :]], axis=0).astype(BF16)

    def unfolded(a):
        a = a.astype(F32)
        return jnp.concatenate([a[:8], a[8:]], axis=1)

    pack_out[0] = folded(jnp.where(row8 < 4, pltpu.roll(packed[:8], 4, 0), packed[8:]))
    pack_out[1] = folded(jnp.where(row8 < 4, packed[:8], pltpu.roll(packed[8:], 4, 0)))
    four = jnp.where(row8 < 4, pltpu.roll(packed[:8], 6, 0), pltpu.roll(packed[8:], 2, 0))
    own_cols[...] = folded(four)

    one = jnp.int32(1)
    pl.semaphore_wait(
        barrier,
        one
        + jnp.where(sends_far, 1, 0)
        + jnp.where(has_left, 1, 0)
        + jnp.where(has_right, 1, 0),
    )
    @pl.when(has_left)
    def _():
        to_left.start()

    @pl.when(has_right)
    def _():
        to_right.start()

    cols_near = remote(own_cols, cols_in.at[1, odd], cols_s.at[0], cols_r.at[0], (partner, cj))
    cols_far = remote(cols_in.at[1, even], cols_in.at[1, odd], cols_s.at[1], cols_r.at[1], (ahead, cj))
    cols_near.start()
    for k in range(FIRST):
        near(k).start()

    held = jnp.logical_or(cj == nc // 2 - 1, cj == nc // 2)

    @pl.when(jnp.logical_not(held))
    def _():
        for k in range(FIRST, CHUNKS):
            near(k).start()

    def passed(far_too, slot):
        return (
            remote(
                cols_in.at[1, slot],
                cols_in.at[2, slot],
                cols_s.at[2 + far_too],
                cols_r.at[2 + far_too],
                (vi, left),
            ),
            remote(
                cols_in.at[1, slot],
                cols_in.at[0, slot],
                cols_s.at[4 + far_too],
                cols_r.at[4 + far_too],
                (vi, right),
            ),
        )

    near_left, near_right = passed(0, even)
    far_left, far_right = passed(1, odd)

    @pl.when(at_top)
    def _():
        got[0, 0] = fv[0]
        got[0, 1] = jnp.zeros((V, Y, X), BF16)

    @pl.when(at_bottom)
    def _():
        got[1, 0] = jnp.zeros((V, Y, X), BF16)
        got[1, 1] = fv[1]

    def lanes(a, k):
        return pltpu.roll(a, (-k) % a.shape[-1], a.ndim - 1)

    def smooth_lanes(a):
        pair = a + lanes(a, -1)
        return pair + lanes(pair, 1)

    def horizontal(i, carry):
        before, last = carry
        u = i // H_STEPS
        v0 = lax.rem(i, H_STEPS) * H_CHUNK
        top = v0 == 0
        before = [jnp.where(top, 0.0, c) for c in before]
        last = [jnp.where(top, 0.0, c) for c in last]
        here = fv[u, pl.ds(v0, H_CHUNK)].astype(F32)
        full[u, pl.ds(v0, H_CHUNK)] = here
        above = jnp.where(top, 0.0, fv[u, jnp.maximum(v0 - 1, 0)].astype(F32))
        below = jnp.where(
            v0 + H_CHUNK < V, fv[u, jnp.minimum(v0 + H_CHUNK, V - 1)].astype(F32), 0.0
        )
        mid_x = jnp.concatenate([above[None], here, below[None]], 0)
        left_x, right_x = lanes(mid_x, -1), lanes(mid_x, 1)
        grad_v = [a[2:] - a[:-2] for a in (left_x, mid_x, right_x)]
        grad_x = [here - lanes(here, -2), right_x[1:-1] - left_x[1:-1], lanes(here, 2) - here]

        def smooth_x(p, q):
            a, b, c = (s * t for s, t in zip(p, q))
            return (a + c) + (b + b)

        now = [smooth_x(grad_v, grad_v), smooth_x(grad_v, grad_x), smooth_x(grad_x, grad_x)]
        run = [jnp.concatenate([a[None], b[None], c], 0) for a, b, c in zip(before, last, now)]
        pairs = [c[1:] + c[:-1] for c in run]
        w, m = weighted(*(c[1:] + c[:-1] for c in pairs))
        weight[u, pl.ds(v0, H_CHUNK)] = w
        moment[u, pl.ds(v0, H_CHUNK)] = m

        @pl.when(v0 == V - H_CHUNK)
        def _():
            w, m = weighted(*(c[-1] + d[-1] for c, d in zip(pairs, now)))
            weight[u, V] = w
            moment[u, V] = m

        return [c[H_CHUNK - 2] for c in now], [c[H_CHUNK - 1] for c in now]

    zeros = [jnp.zeros((Y, X), F32)] * 3
    lax.fori_loop(0, 2 * H_STEPS, horizontal, (zeros, zeros))

    cols_near.wait_recv()

    @pl.when(sends_far)
    def _():
        cols_far.start()

    @pl.when(has_left)
    def _():
        near_left.start()

    @pl.when(has_right)
    def _():
        near_right.start()

    @pl.when(held)
    def _():
        for k in range(FIRST, FLIGHT):
            near(k).start()

    def relay(k):
        near_in(k).wait_recv()

        @pl.when(jnp.logical_and(held, k + FLIGHT < CHUNKS))
        def _():
            near(k + FLIGHT).start()

        @pl.when(sends_far)
        def _():
            far(k).start()


    lane = lax.broadcasted_iota(jnp.int32, (STEP, 8, X), 2)
    sub = lax.broadcasted_iota(jnp.int32, (STEP, 8, X), 1)
    rim = jnp.logical_or(lane < 2, lane >= X - 2)
    outer = jnp.logical_or(lane == 0, lane == X - 1)

    def parts(ref, *at):
        return [ref[(*at, pl.ds(p, 8, stride=4), slice(None))] for p in range(4)]

    def y_up(a, rest=0.0):
        return a[1:] + [jnp.where(sub == 7, rest, pltpu.roll(a[0], 7, 1))]

    def y_down(a):
        return [jnp.where(sub == 0, 0.0, pltpu.roll(a[3], 1, 1))] + a[:3]

    def smooth_y(a):
        pair = [b + c for b, c in zip(a, y_down(a))]
        return [b + c for b, c in zip(pair, y_up(pair, a[3]))]

    def vertical(v0):
        span = pl.ds(v0, STEP)
        for slot in range(2):
            for u in range(ROWS):
                wide[2 * slot + u] = got[slot, u, span].astype(F32)
        every = slice(None)
        field = (
            [parts(wide, 0, every), parts(wide, 1, every)]
            + [parts(full, u, span) for u in range(ROWS)]
            + [parts(wide, 2, every), parts(wide, 3, every)]
        )
        comps = []
        for r in range(1, 5):
            grad_u = [a - b for a, b in zip(field[r + 1], field[r - 1])]
            grad_y = [a - b for a, b in zip(y_up(field[r]), y_down(field[r]))]
            comps.append(
                [
                    [a * b for a, b in zip(g, h)]
                    for g, h in ((grad_u, grad_u), (grad_u, grad_y), (grad_y, grad_y))
                ]
            )
        pairs = [
            [[a + b for a, b in zip(c, d)] for c, d in zip(comps[r], comps[r + 1])] for r in range(3)
        ]
        for u in range(ROWS):
            tensor = [
                smooth_y([a + b for a, b in zip(c, d)]) for c, d in zip(pairs[u], pairs[u + 1])
            ]
            past = pl.ds(v0 + 1, STEP)
            w, m = parts(weight, u, past), parts(moment, u, past)
            for p in range(4):
                slope[u, span, p] = join(w[p], m[p], *(c[p] for c in tensor))

    def variation(v0):
        span = pl.ds(v0, STEP)
        for u in range(ROWS):
            t = parts(fix, u, span)
            joined = [jnp.where(rim, t[p], slope[u, span, p]) for p in range(4)]
            flux_x, flux_y = [], []
            for here, below in zip(joined, y_up(joined)):
                step_x = lanes(here, 1) - here
                step_y = below - here
                scale = lax.rsqrt(step_x * step_x + step_y * step_y + 1.0)
                flux_x.append(step_x * scale)
                flux_y.append(step_y * scale)
            for p, above in enumerate(y_down(flux_y)):
                depth = joined[p] + 0.2 * (flux_x[p] - lanes(flux_x[p], -1) + flux_y[p] - above)
                out[u, span, pl.ds(p, 8, stride=4), :] = jnp.where(outer, lanes(t[p], -63), depth)

    place = lax.broadcasted_iota(jnp.int32, (8, PLANE), 1)
    y_at = lax.rem(place, Y)

    def cols_by(a, k):
        return pltpu.roll(a, (-k) % 8, 0)

    def y_by(a, k):
        return jnp.where(y_at == (Y - 1 if k > 0 else 0), 0.0, pltpu.roll(a, (-k) % PLANE, 1))

    def v_by(a, k):
        return jnp.where(
            place >= PLANE - Y if k > 0 else place < Y, 0.0, pltpu.roll(a, (-k * Y) % PLANE, 1)
        )

    def smooth_by(by, a):
        return by(a, -1) + (a + a) + by(a, 1)

    relay(0)
    relay(1)
    relay(2)

    @pl.when(has_left)
    def _():
        to_right.wait_recv()

    @pl.when(has_right)
    def _():
        to_left.wait_recv()

    first, final = cj == 0, cj == nc - 1
    own = pack[...].astype(F32)
    from_l = unfolded(pack_l[...])
    from_r = unfolded(pack_r[...])
    for u in range(ROWS):
        mine = own[8 * u : 8 * u + 8]
        l_in = pltpu.roll(from_l, 4, 0) if u else from_l
        r_in = from_r if u else pltpu.roll(from_r, 4, 0)
        flip_l = jnp.where(row8 == 2, pltpu.roll(mine, 6, 0), 0.0)
        flip_r = jnp.where(row8 == 5, pltpu.roll(mine, 2, 0), 0.0)
        l_in = jnp.where(first, flip_l, l_in)
        r_in = jnp.where(final, flip_r, r_in)
        e_l = jnp.where(row8 < 4, l_in, mine)
        e_r = jnp.where(row8 < 4, mine, r_in)
        edge[0, 2 + u] = e_l
        edge[1, 2 + u] = e_r

    def edges_h(side, carry):
        for u in range(ROWS):
            f = edge[side, 2 + u]
            grad_v = v_by(f, 1) - v_by(f, -1)
            grad_x = cols_by(f, 1) - cols_by(f, -1)
            w, m = weighted(
                *(
                    smooth_by(v_by, smooth_by(cols_by, c))
                    for c in (grad_v * grad_v, grad_v * grad_x, grad_x * grad_x)
                )
            )
            edge_j[side, u] = w
            edge_d[side, u] = m
        relay(3 + side)
        return carry

    lax.fori_loop(0, 2, edges_h, 0)

    @pl.when(has_far)
    def _():
        cols_far.wait_recv()

        @pl.when(has_left)
        def _():
            far_left.start()

        @pl.when(has_right)
        def _():
            far_right.start()

    relay(5)

    def arrived(g):
        @pl.when(has_far)
        def _():
            both = pl.ds(g * STEP, STEP)
            remote(
                got.at[even, :, both], got.at[odd, :, both], far_s, far_r.at[g], (ahead, cj)
            ).wait_recv()

    def start(g, carry):
        relay(2 * g + 6)
        relay(2 * g + 7)
        arrived(g)
        vertical(g * STEP)
        return carry

    lax.fori_loop(0, BEFORE, start, 0)

    @pl.when(has_left)
    def _():
        near_right.wait_recv()

        @pl.when(has_far)
        def _():
            far_right.wait_recv()

    @pl.when(has_right)
    def _():
        near_left.wait_recv()

        @pl.when(has_far)
        def _():
            far_left.wait_recv()

    for slot in range(2):
        from_l, here, from_r = (
            unfolded(cols_in[origin, slot]) for origin in range(3)
        )
        for u in range(ROWS):
            with_l = jnp.where(row8 == 4 * u + 1, from_l, here)
            with_r = jnp.where(row8 == 4 * u + 2, from_r, here)
            edge[0, 4 * slot + u] = pltpu.roll(with_l, 2 + 4 * u, 0)
            edge[1, 4 * slot + u] = pltpu.roll(with_r, 2 + 4 * u, 0)

    @pl.when(at_top)
    def _():
        for side in range(2):
            edge[side, 0] = edge[side, 2]
            edge[side, 1] = jnp.zeros((8, PLANE), F32)

    @pl.when(at_bottom)
    def _():
        for side in range(2):
            edge[side, 4] = jnp.zeros((8, PLANE), F32)
            edge[side, 5] = edge[side, 3]

    def edges(side, carry):
        j_below = jnp.where(jnp.logical_and(final, side == 1), 4, 8)
        q_from = jnp.where(jnp.logical_and(first, side == 0), 4, 0)
        tiles = [edge[side, r] for r in range(6)]
        comps = []
        for r in range(1, 5):
            grad_u = tiles[r + 1] - tiles[r - 1]
            grad_y = y_by(tiles[r], 1) - y_by(tiles[r], -1)
            comps.append((grad_u * grad_u, grad_u * grad_y, grad_y * grad_y))
        for u in range(ROWS):
            w, m = edge_j[side, u], edge_d[side, u]
            tensor = [
                smooth_by(y_by, a + (b + b) + c) for a, b, c in zip(comps[u], comps[u + 1], comps[u + 2])
            ]
            joined = jnp.where(row8 < j_below, join(w, m, *tensor), 0.0)
            step_x = cols_by(joined, 1) - joined
            step_y = y_by(joined, 1) - joined
            scale = lax.rsqrt(step_x * step_x + step_y * step_y + 1.0)
            flux_x = jnp.where(row8 >= q_from, step_x * scale, 0.0)
            flux_y = step_y * scale
            depth = joined + 0.2 * (flux_x - cols_by(flux_x, -1) + flux_y - y_by(flux_y, -1))
            edge_j[side, u] = pltpu.roll(joined, 4, 0)
            edge_d[side, u] = pltpu.roll(depth, 5, 0)
        relay(2 * BEFORE + 6 + side)
        return carry

    lax.fori_loop(0, 2, edges, 0)

    small = lax.broadcasted_iota(jnp.int32, (8, X), 0)

    def spread_out(u, carry):
        for b in range(PLANE // X):
            part = pl.ds(b * X, X)
            both = jnp.where(small == 0, edge_d[1, u, :, part], edge_d[0, u, :, part])
            block = jnp.concatenate(
                [
                    edge_j[0, u, :, part],
                    jnp.zeros((56, X), F32),
                    both,
                    jnp.zeros((48, X), F32),
                    edge_j[1, u, :, part],
                ],
                axis=0,
            )
            fix[u, pl.ds(4 * b, 4)] = block.T.reshape(4, Y, X)
        return carry

    lax.fori_loop(0, 2, spread_out, 0)

    def finish(g, carry):
        for k in range(2):

            @pl.when(2 * g + k + 8 < CHUNKS)
            def _():
                relay(2 * g + k + 8)

        def varied(i, c):
            variation(i * STEP)
            return c

        lax.fori_loop(jnp.where(g == BEFORE, 0, g - 1), g, varied, 0)
        arrived(g)
        vertical(g * STEP)
        return carry

    lax.fori_loop(BEFORE, V // STEP, finish, 0)
    variation(V - STEP)

    @pl.when(has_left)
    def _():
        to_left.wait_send()
        near_left.wait_send()

    @pl.when(has_right)
    def _():
        to_right.wait_send()
        near_right.wait_send()

    @pl.when(jnp.logical_and(has_left, has_far))
    def _():
        far_left.wait_send()

    @pl.when(jnp.logical_and(has_right, has_far))
    def _():
        far_right.wait_send()

    cols_near.wait_send()
    remote(f_hbm, got.at[odd], near_s, near_r.at[0], (partner, cj)).wait_send()

    @pl.when(sends_far)
    def _():
        cols_far.wait_send()
        remote(got.at[even], got.at[odd], far_s, far_r.at[0], (ahead, cj)).wait_send()


def local(nv, nc, light_field):
    block = (ROWS, V, Y, X)
    dma = pltpu.SemaphoreType.DMA
    return pl.pallas_call(
        functools.partial(kernel, nv, nc),
        out_shape=jax.ShapeDtypeStruct(block, F32),
        in_specs=[pl.BlockSpec(memory_space=pl.ANY)],
        out_specs=pl.BlockSpec(memory_space=pltpu.VMEM),
        scratch_shapes=[
            pltpu.VMEM(block, BF16),
            pltpu.VMEM(block, F32),
            pltpu.VMEM((2, *block), BF16),
            pltpu.VMEM((4, STEP, Y, X), F32),
            pltpu.VMEM((ROWS, V + 1, Y, X), F32),
            pltpu.VMEM((ROWS, V + 1, Y, X), F32),
            pltpu.VMEM(block, F32),
            pltpu.VMEM((ROWS, V, 4, 8, X), F32),
            pltpu.VMEM((16, PLANE), BF16),
            pltpu.VMEM((2, 16, PLANE // 2), BF16),
            pltpu.VMEM((16, PLANE // 2), BF16),
            pltpu.VMEM((16, PLANE // 2), BF16),
            pltpu.VMEM((16, PLANE // 2), BF16),
            pltpu.VMEM((3, 2, 16, PLANE // 2), BF16),
            pltpu.VMEM((2, 6, 8, PLANE), F32),
            pltpu.VMEM((2, ROWS, 8, PLANE), F32),
            pltpu.VMEM((2, ROWS, 8, PLANE), F32),
            dma,
            dma,
            dma((CHUNKS,)),
            dma,
            dma((CHUNKS // 2,)),
            dma((2,)),
            dma((2,)),
            dma((6,)),
            dma((6,)),
        ],
        compiler_params=pltpu.CompilerParams(
            collective_id=0, has_side_effects=True, vmem_limit_bytes=32 << 20
        ),
        cost_estimate=pl.CostEstimate(flops=60_000_000, bytes_accessed=1_600_000, transcendentals=800_000),
    )(pltpu.with_memory_space_constraint(light_field, pltpu.HBM))


def solution(mesh):
    return jax.shard_map(
        functools.partial(local, mesh.shape["views"], mesh.shape["cols"]),
        mesh=mesh,
        in_specs=(P("views", None, None, "cols"),),
        out_specs=P("views", None, None, "cols"),
        check_vma=False,
    )
```

```python
import functools

import jax
import jax.numpy as jnp
from jax import lax
from jax.experimental import pallas as pl
from jax.experimental.pallas import tpu as pltpu
from jax.sharding import PartitionSpec as P

MESH = pl.DeviceIdType.MESH
F32 = jnp.float32
BF16 = jnp.bfloat16
ROWS, V, Y, X = 2, 32, 32, 128
CHUNK = 2
CHUNKS = V // CHUNK
STEP = 4
H_CHUNK = 8
H_STEPS = V // H_CHUNK
BEFORE = 3
FIRST = 6
SECOND = 11
PLANE = V * Y


def recip(x):
    r = pl.reciprocal(x, approx=True)
    return r * (2.0 - x * r)


def measures(first, cross, second):
    apart = second - first
    whole = second + first
    twice = cross + cross
    return apart * apart + twice * twice, whole * whole + 4096.0, cross, second + 64.0


def weighted(first, cross, second):
    spread, energy, cross, pivot = measures(first, cross, second)
    part = spread * recip(energy * pivot)
    return part * pivot + 0.1, part * cross


def join(weight_h, moment_h, first, cross, second):
    spread, energy, cross, pivot = measures(first, cross, second)
    above = moment_h * (energy * pivot) + spread * cross
    below = pivot * (energy * weight_h + spread)
    return -(above * recip(below))


def kernel(
    nv,
    nc,
    f_hbm,
    out,
    fv,
    full,
    got,
    wide,
    weight,
    moment,
    fix,
    slope,
    pack,
    pack_out,
    pack_l,
    pack_r,
    own_cols,
    cols_in,
    edge,
    edge_j,
    edge_d,
    load_sem,
    near_s,
    near_r,
    far_s,
    far_r,
    pack_s,
    pack_rs,
    cols_s,
    cols_r,
    ready,
):
    vi = lax.axis_index("views")
    cj = lax.axis_index("cols")
    odd = lax.rem(vi, 2)
    even = 1 - odd
    partner = vi + 1 - 2 * odd
    ahead = lax.rem(vi + nv + 2 - 4 * odd, nv)
    behind = lax.rem(vi + nv - 2 + 4 * odd, nv)
    left = lax.rem(cj + nc - 1, nc)
    right = lax.rem(cj + 1, nc)
    at_top = vi == 0
    at_bottom = vi == nv - 1
    has_far = jnp.logical_and(vi > 0, vi < nv - 1)
    sends_far = jnp.logical_and(vi != nv - 2, vi != 1)

    barrier = pltpu.get_barrier_semaphore()
    has_left, has_right = cj > 0, cj < nc - 1

    def greet(there):
        pl.semaphore_signal(barrier, inc=1, device_id=there, device_id_type=MESH)

    middle = nc // 2
    is_even = lax.rem(cj, 2) == 0
    late_l = jnp.logical_and(has_left, jnp.logical_and(is_even, cj != middle))
    late_r = jnp.logical_and(has_right, jnp.logical_or(is_even, cj == middle - 1))
    early_l = jnp.logical_and(has_left, jnp.logical_not(late_l))
    early_r = jnp.logical_and(has_right, jnp.logical_not(late_r))
    late_z = jnp.logical_and(has_far, odd == 0)
    early_z = jnp.logical_and(sends_far, odd == 0)
    late_q = jnp.logical_and(sends_far, odd == 1)
    early_q = jnp.logical_and(has_far, odd == 1)

    greet((partner, cj))
    for exists, there in (
        (early_z, (ahead, cj)),
        (early_q, (behind, cj)),
        (early_l, (vi, left)),
        (early_r, (vi, right)),
    ):

        @pl.when(exists)
        def _():
            greet(there)

    load = pltpu.make_async_copy(f_hbm, fv, load_sem)
    load.start()

    def remote(src, dst, s, r, there):
        return pltpu.make_async_remote_copy(
            src_ref=src, dst_ref=dst, send_sem=s, recv_sem=r, device_id=there, device_id_type=MESH
        )

    def near(k):
        span = pl.ds(k * CHUNK, CHUNK)
        return remote(f_hbm.at[:, span], got.at[odd, :, span], near_s, near_r.at[k], (partner, cj))

    def near_in(k):
        span = pl.ds(k * CHUNK, CHUNK)
        return remote(f_hbm.at[:, span], got.at[even, :, span], near_s, near_r.at[k], (partner, cj))

    def far(k):
        span = pl.ds(k * CHUNK, CHUNK)
        return remote(got.at[even, :, span], got.at[odd, :, span], far_s, far_r.at[k // 2], (ahead, cj))

    to_left = remote(pack_out.at[0], pack_r, pack_s.at[0], pack_rs.at[0], (vi, left))
    to_right = remote(pack_out.at[1], pack_l, pack_s.at[1], pack_rs.at[1], (vi, right))

    load.wait()

    row8 = lax.broadcasted_iota(jnp.int32, (8, PLANE), 0)
    row16 = lax.broadcasted_iota(jnp.int32, (16, X), 0)
    lane16 = lax.broadcasted_iota(jnp.int32, (16, X), 1)
    r8 = lax.rem(row16, 8)
    wanted = jnp.where(r8 < 4, r8 + (X - 4), r8 - 4)

    packed = jnp.zeros((16, PLANE), F32)
    for u in range(ROWS):
        pick = jnp.where(jnp.logical_and(lane16 == wanted, row16 // 8 == u), 1.0, 0.0).astype(BF16)
        packed = packed + lax.dot_general(
            pick, fv[u].reshape(PLANE, X), (((1,), (1,)), ((), ())), preferred_element_type=F32
        )
    pack[...] = packed.astype(BF16)

    def folded(a):
        return jnp.concatenate([a[:, : PLANE // 2], a[:, PLANE // 2 :]], axis=0).astype(BF16)

    def unfolded(a):
        a = a.astype(F32)
        return jnp.concatenate([a[:8], a[8:]], axis=1)

    pack_out[0] = folded(jnp.where(row8 < 4, pltpu.roll(packed[:8], 4, 0), packed[8:]))
    pack_out[1] = folded(jnp.where(row8 < 4, packed[:8], pltpu.roll(packed[8:], 4, 0)))
    four = jnp.where(row8 < 4, pltpu.roll(packed[:8], 6, 0), pltpu.roll(packed[8:], 2, 0))
    own_cols[...] = folded(four)

    greeted = jnp.int32(1)
    for late in (late_z, late_q, late_l, late_r):
        greeted = greeted + jnp.where(late, 1, 0)
    pl.semaphore_wait(barrier, greeted)

    def tell(which, there):
        pl.semaphore_signal(ready.at[which], inc=1, device_id=there, device_id_type=MESH)

    @pl.when(late_l)
    def _():
        to_left.start()
        tell(1, (vi, left))

    @pl.when(late_r)
    def _():
        to_right.start()
        tell(0, (vi, right))

    @pl.when(late_z)
    def _():
        tell(2, (behind, cj))

    cols_near = remote(own_cols, cols_in.at[1, odd], cols_s.at[0], cols_r.at[0], (partner, cj))
    cols_far = remote(cols_in.at[1, even], cols_in.at[1, odd], cols_s.at[1], cols_r.at[1], (ahead, cj))
    cols_near.start()
    for k in range(FIRST):
        near(k).start()

    held = jnp.logical_or(cj == nc // 2 - 1, cj == nc // 2)

    @pl.when(jnp.logical_not(held))
    def _():
        for k in range(FIRST, CHUNKS):
            near(k).start()

    def passed(far_too, slot):
        return (
            remote(
                cols_in.at[1, slot],
                cols_in.at[2, slot],
                cols_s.at[2 + far_too],
                cols_r.at[2 + far_too],
                (vi, left),
            ),
            remote(
                cols_in.at[1, slot],
                cols_in.at[0, slot],
                cols_s.at[4 + far_too],
                cols_r.at[4 + far_too],
                (vi, right),
            ),
        )

    near_left, near_right = passed(0, even)
    far_left, far_right = passed(1, odd)

    @pl.when(at_top)
    def _():
        got[0, 0] = fv[0]
        got[0, 1] = jnp.zeros((V, Y, X), BF16)

    @pl.when(at_bottom)
    def _():
        got[1, 0] = jnp.zeros((V, Y, X), BF16)
        got[1, 1] = fv[1]

    def lanes(a, k):
        return pltpu.roll(a, (-k) % a.shape[-1], a.ndim - 1)

    def smooth_lanes(a):
        pair = a + lanes(a, -1)
        return pair + lanes(pair, 1)

    def horizontal(i, carry):
        before, last = carry
        u = i // H_STEPS
        v0 = lax.rem(i, H_STEPS) * H_CHUNK
        top = v0 == 0
        before = [jnp.where(top, 0.0, c) for c in before]
        last = [jnp.where(top, 0.0, c) for c in last]
        here = fv[u, pl.ds(v0, H_CHUNK)].astype(F32)
        full[u, pl.ds(v0, H_CHUNK)] = here
        above = jnp.where(top, 0.0, fv[u, jnp.maximum(v0 - 1, 0)].astype(F32))
        below = jnp.where(
            v0 + H_CHUNK < V, fv[u, jnp.minimum(v0 + H_CHUNK, V - 1)].astype(F32), 0.0
        )
        mid_x = jnp.concatenate([above[None], here, below[None]], 0)
        left_x, right_x = lanes(mid_x, -1), lanes(mid_x, 1)
        grad_v = [a[2:] - a[:-2] for a in (left_x, mid_x, right_x)]
        grad_x = [here - lanes(here, -2), right_x[1:-1] - left_x[1:-1], lanes(here, 2) - here]

        def smooth_x(p, q):
            a, b, c = (s * t for s, t in zip(p, q))
            return (a + c) + (b + b)

        now = [smooth_x(grad_v, grad_v), smooth_x(grad_v, grad_x), smooth_x(grad_x, grad_x)]
        run = [jnp.concatenate([a[None], b[None], c], 0) for a, b, c in zip(before, last, now)]
        pairs = [c[1:] + c[:-1] for c in run]
        w, m = weighted(*(c[1:] + c[:-1] for c in pairs))
        weight[u, pl.ds(v0, H_CHUNK)] = w
        moment[u, pl.ds(v0, H_CHUNK)] = m

        @pl.when(v0 == V - H_CHUNK)
        def _():
            w, m = weighted(*(c[-1] + d[-1] for c, d in zip(pairs, now)))
            weight[u, V] = w
            moment[u, V] = m

        return [c[H_CHUNK - 2] for c in now], [c[H_CHUNK - 1] for c in now]

    zeros = [jnp.zeros((Y, X), F32)] * 3
    lax.fori_loop(0, 2 * H_STEPS, horizontal, (zeros, zeros))

    @pl.when(early_l)
    def _():
        pl.semaphore_wait(ready.at[0], 1)
        to_left.start()

    @pl.when(early_r)
    def _():
        pl.semaphore_wait(ready.at[1], 1)
        to_right.start()

    @pl.when(early_z)
    def _():
        pl.semaphore_wait(ready.at[2], 1)

    cols_near.wait_recv()

    @pl.when(sends_far)
    def _():
        cols_far.start()

    @pl.when(has_left)
    def _():
        near_left.start()

    @pl.when(has_right)
    def _():
        near_right.start()

    @pl.when(held)
    def _():
        for k in range(FIRST, SECOND):
            near(k).start()

    def relay(k):
        near_in(k).wait_recv()

        @pl.when(sends_far)
        def _():
            far(k).start()


    lane = lax.broadcasted_iota(jnp.int32, (STEP, 8, X), 2)
    sub = lax.broadcasted_iota(jnp.int32, (STEP, 8, X), 1)
    rim = jnp.logical_or(lane < 2, lane >= X - 2)
    outer = jnp.logical_or(lane == 0, lane == X - 1)

    def parts(ref, *at):
        return [ref[(*at, pl.ds(p, 8, stride=4), slice(None))] for p in range(4)]

    def y_up(a, rest=0.0):
        return a[1:] + [jnp.where(sub == 7, rest, pltpu.roll(a[0], 7, 1))]

    def y_down(a):
        return [jnp.where(sub == 0, 0.0, pltpu.roll(a[3], 1, 1))] + a[:3]

    def smooth_y(a):
        pair = [b + c for b, c in zip(a, y_down(a))]
        return [b + c for b, c in zip(pair, y_up(pair, a[3]))]

    def vertical(v0):
        span = pl.ds(v0, STEP)
        for slot in range(2):
            for u in range(ROWS):
                wide[2 * slot + u] = got[slot, u, span].astype(F32)
        every = slice(None)
        field = (
            [parts(wide, 0, every), parts(wide, 1, every)]
            + [parts(full, u, span) for u in range(ROWS)]
            + [parts(wide, 2, every), parts(wide, 3, every)]
        )
        comps = []
        for r in range(1, 5):
            grad_u = [a - b for a, b in zip(field[r + 1], field[r - 1])]
            grad_y = [a - b for a, b in zip(y_up(field[r]), y_down(field[r]))]
            comps.append(
                [
                    [a * b for a, b in zip(g, h)]
                    for g, h in ((grad_u, grad_u), (grad_u, grad_y), (grad_y, grad_y))
                ]
            )
        pairs = [
            [[a + b for a, b in zip(c, d)] for c, d in zip(comps[r], comps[r + 1])] for r in range(3)
        ]
        for u in range(ROWS):
            tensor = [
                smooth_y([a + b for a, b in zip(c, d)]) for c, d in zip(pairs[u], pairs[u + 1])
            ]
            past = pl.ds(v0 + 1, STEP)
            w, m = parts(weight, u, past), parts(moment, u, past)
            for p in range(4):
                slope[u, span, p] = join(w[p], m[p], *(c[p] for c in tensor))

    def variation(v0):
        span = pl.ds(v0, STEP)
        for u in range(ROWS):
            t = parts(fix, u, span)
            joined = [jnp.where(rim, t[p], slope[u, span, p]) for p in range(4)]
            flux_x, flux_y = [], []
            for here, below in zip(joined, y_up(joined)):
                step_x = lanes(here, 1) - here
                step_y = below - here
                scale = lax.rsqrt(step_x * step_x + step_y * step_y + 1.0)
                flux_x.append(step_x * scale)
                flux_y.append(step_y * scale)
            for p, above in enumerate(y_down(flux_y)):
                depth = joined[p] + 0.2 * (flux_x[p] - lanes(flux_x[p], -1) + flux_y[p] - above)
                out[u, span, pl.ds(p, 8, stride=4), :] = jnp.where(outer, lanes(t[p], -63), depth)

    place = lax.broadcasted_iota(jnp.int32, (8, PLANE), 1)
    y_at = lax.rem(place, Y)

    def cols_by(a, k):
        return pltpu.roll(a, (-k) % 8, 0)

    def y_by(a, k):
        return jnp.where(y_at == (Y - 1 if k > 0 else 0), 0.0, pltpu.roll(a, (-k) % PLANE, 1))

    def v_by(a, k):
        return jnp.where(
            place >= PLANE - Y if k > 0 else place < Y, 0.0, pltpu.roll(a, (-k * Y) % PLANE, 1)
        )

    def smooth_by(by, a):
        return by(a, -1) + (a + a) + by(a, 1)

    for k in range(4):
        relay(k)

    @pl.when(has_far)
    def _():
        cols_far.wait_recv()

        @pl.when(has_left)
        def _():
            far_left.start()

        @pl.when(has_right)
        def _():
            far_right.start()

    @pl.when(held)
    def _():
        for k in range(SECOND, CHUNKS):
            near(k).start()

    relay(4)
    @pl.when(has_left)
    def _():
        to_right.wait_recv()

    @pl.when(has_right)
    def _():
        to_left.wait_recv()

    first, final = cj == 0, cj == nc - 1
    own = pack[...].astype(F32)
    from_l = unfolded(pack_l[...])
    from_r = unfolded(pack_r[...])
    for u in range(ROWS):
        mine = own[8 * u : 8 * u + 8]
        l_in = pltpu.roll(from_l, 4, 0) if u else from_l
        r_in = from_r if u else pltpu.roll(from_r, 4, 0)
        flip_l = jnp.where(row8 == 2, pltpu.roll(mine, 6, 0), 0.0)
        flip_r = jnp.where(row8 == 5, pltpu.roll(mine, 2, 0), 0.0)
        l_in = jnp.where(first, flip_l, l_in)
        r_in = jnp.where(final, flip_r, r_in)
        e_l = jnp.where(row8 < 4, l_in, mine)
        e_r = jnp.where(row8 < 4, mine, r_in)
        edge[0, 2 + u] = e_l
        edge[1, 2 + u] = e_r

    def edges_h(side, carry):
        for u in range(ROWS):
            f = edge[side, 2 + u]
            grad_v = v_by(f, 1) - v_by(f, -1)
            grad_x = cols_by(f, 1) - cols_by(f, -1)
            w, m = weighted(
                *(
                    smooth_by(v_by, smooth_by(cols_by, c))
                    for c in (grad_v * grad_v, grad_v * grad_x, grad_x * grad_x)
                )
            )
            edge_j[side, u] = w
            edge_d[side, u] = m
        relay(5 + side)
        return carry

    lax.fori_loop(0, 2, edges_h, 0)


    def arrived(g):
        @pl.when(has_far)
        def _():
            both = pl.ds(g * STEP, STEP)
            remote(
                got.at[even, :, both], got.at[odd, :, both], far_s, far_r.at[g], (ahead, cj)
            ).wait_recv()

    def start(g, carry):
        @pl.when(g > 0)
        def _():
            relay(2 * g + 6)

        relay(2 * g + 7)
        arrived(g)
        vertical(g * STEP)
        return carry

    lax.fori_loop(0, BEFORE, start, 0)

    @pl.when(has_left)
    def _():
        near_right.wait_recv()

        @pl.when(has_far)
        def _():
            far_right.wait_recv()

    @pl.when(has_right)
    def _():
        near_left.wait_recv()

        @pl.when(has_far)
        def _():
            far_left.wait_recv()

    for slot in range(2):
        from_l, here, from_r = (
            unfolded(cols_in[origin, slot]) for origin in range(3)
        )
        for u in range(ROWS):
            with_l = jnp.where(row8 == 4 * u + 1, from_l, here)
            with_r = jnp.where(row8 == 4 * u + 2, from_r, here)
            edge[0, 4 * slot + u] = pltpu.roll(with_l, 2 + 4 * u, 0)
            edge[1, 4 * slot + u] = pltpu.roll(with_r, 2 + 4 * u, 0)

    @pl.when(at_top)
    def _():
        for side in range(2):
            edge[side, 0] = edge[side, 2]
            edge[side, 1] = jnp.zeros((8, PLANE), F32)

    @pl.when(at_bottom)
    def _():
        for side in range(2):
            edge[side, 4] = jnp.zeros((8, PLANE), F32)
            edge[side, 5] = edge[side, 3]

    def edges(side, carry):
        j_below = jnp.where(jnp.logical_and(final, side == 1), 4, 8)
        q_from = jnp.where(jnp.logical_and(first, side == 0), 4, 0)
        tiles = [edge[side, r] for r in range(6)]
        comps = []
        for r in range(1, 5):
            grad_u = tiles[r + 1] - tiles[r - 1]
            grad_y = y_by(tiles[r], 1) - y_by(tiles[r], -1)
            comps.append((grad_u * grad_u, grad_u * grad_y, grad_y * grad_y))
        for u in range(ROWS):
            w, m = edge_j[side, u], edge_d[side, u]
            tensor = [
                smooth_by(y_by, a + (b + b) + c) for a, b, c in zip(comps[u], comps[u + 1], comps[u + 2])
            ]
            joined = jnp.where(row8 < j_below, join(w, m, *tensor), 0.0)
            step_x = cols_by(joined, 1) - joined
            step_y = y_by(joined, 1) - joined
            scale = lax.rsqrt(step_x * step_x + step_y * step_y + 1.0)
            flux_x = jnp.where(row8 >= q_from, step_x * scale, 0.0)
            flux_y = step_y * scale
            depth = joined + 0.2 * (flux_x - cols_by(flux_x, -1) + flux_y - y_by(flux_y, -1))
            edge_j[side, u] = pltpu.roll(joined, 4, 0)
            edge_d[side, u] = pltpu.roll(depth, 5, 0)
        relay(2 * BEFORE + 6 + side)
        return carry

    lax.fori_loop(0, 2, edges, 0)

    small = lax.broadcasted_iota(jnp.int32, (8, X), 0)

    def spread_out(u, carry):
        for b in range(PLANE // X):
            part = pl.ds(b * X, X)
            both = jnp.where(small == 0, edge_d[1, u, :, part], edge_d[0, u, :, part])
            block = jnp.concatenate(
                [
                    edge_j[0, u, :, part],
                    jnp.zeros((56, X), F32),
                    both,
                    jnp.zeros((48, X), F32),
                    edge_j[1, u, :, part],
                ],
                axis=0,
            )
            fix[u, pl.ds(4 * b, 4)] = block.T.reshape(4, Y, X)
        return carry

    lax.fori_loop(0, 2, spread_out, 0)

    def finish(g, carry):
        for k in range(2):

            @pl.when(2 * g + k + 8 < CHUNKS)
            def _():
                relay(2 * g + k + 8)

        def varied(i, c):
            variation(i * STEP)
            return c

        lax.fori_loop(jnp.where(g == BEFORE, 0, g - 1), g, varied, 0)
        arrived(g)
        vertical(g * STEP)
        return carry

    lax.fori_loop(BEFORE, V // STEP, finish, 0)
    variation(V - STEP)

    @pl.when(has_left)
    def _():
        to_left.wait_send()
        near_left.wait_send()

    @pl.when(has_right)
    def _():
        to_right.wait_send()
        near_right.wait_send()

    @pl.when(jnp.logical_and(has_left, has_far))
    def _():
        far_left.wait_send()

    @pl.when(jnp.logical_and(has_right, has_far))
    def _():
        far_right.wait_send()

    cols_near.wait_send()
    remote(f_hbm, got.at[odd], near_s, near_r.at[0], (partner, cj)).wait_send()

    @pl.when(sends_far)
    def _():
        cols_far.wait_send()
        remote(got.at[even], got.at[odd], far_s, far_r.at[0], (ahead, cj)).wait_send()


def local(nv, nc, light_field):
    block = (ROWS, V, Y, X)
    dma = pltpu.SemaphoreType.DMA
    return pl.pallas_call(
        functools.partial(kernel, nv, nc),
        out_shape=jax.ShapeDtypeStruct(block, F32),
        in_specs=[pl.BlockSpec(memory_space=pl.ANY)],
        out_specs=pl.BlockSpec(memory_space=pltpu.VMEM),
        scratch_shapes=[
            pltpu.VMEM(block, BF16),
            pltpu.VMEM(block, F32),
            pltpu.VMEM((2, *block), BF16),
            pltpu.VMEM((4, STEP, Y, X), F32),
            pltpu.VMEM((ROWS, V + 1, Y, X), F32),
            pltpu.VMEM((ROWS, V + 1, Y, X), F32),
            pltpu.VMEM(block, F32),
            pltpu.VMEM((ROWS, V, 4, 8, X), F32),
            pltpu.VMEM((16, PLANE), BF16),
            pltpu.VMEM((2, 16, PLANE // 2), BF16),
            pltpu.VMEM((16, PLANE // 2), BF16),
            pltpu.VMEM((16, PLANE // 2), BF16),
            pltpu.VMEM((16, PLANE // 2), BF16),
            pltpu.VMEM((3, 2, 16, PLANE // 2), BF16),
            pltpu.VMEM((2, 6, 8, PLANE), F32),
            pltpu.VMEM((2, ROWS, 8, PLANE), F32),
            pltpu.VMEM((2, ROWS, 8, PLANE), F32),
            dma,
            dma,
            dma((CHUNKS,)),
            dma,
            dma((CHUNKS // 2,)),
            dma((2,)),
            dma((2,)),
            dma((6,)),
            dma((6,)),
            pltpu.SemaphoreType.REGULAR((3,)),
        ],
        compiler_params=pltpu.CompilerParams(
            collective_id=0, has_side_effects=True, vmem_limit_bytes=32 << 20
        ),
        cost_estimate=pl.CostEstimate(flops=60_000_000, bytes_accessed=1_600_000, transcendentals=800_000),
    )(pltpu.with_memory_space_constraint(light_field, pltpu.HBM))


def solution(mesh):
    return jax.shard_map(
        functools.partial(local, mesh.shape["views"], mesh.shape["cols"]),
        mesh=mesh,
        in_specs=(P("views", None, None, "cols"),),
        out_specs=P("views", None, None, "cols"),
        check_vma=False,
    )
```

```python
import functools

import jax
import jax.numpy as jnp
from jax import lax
from jax.experimental import pallas as pl
from jax.experimental.pallas import tpu as pltpu
from jax.sharding import PartitionSpec as P

MESH = pl.DeviceIdType.MESH
F32 = jnp.float32
BF16 = jnp.bfloat16
ROWS, V, Y, X = 2, 32, 32, 128
CHUNK = 2
CHUNKS = V // CHUNK
STEP = 4
H_CHUNK = 8
H_STEPS = V // H_CHUNK
BEFORE = 3
FIRST = 6
SECOND = 11
PLANE = V * Y


def recip(x):
    r = pl.reciprocal(x, approx=True)
    return r * (2.0 - x * r)


def measures(first, cross, second):
    apart = second - first
    whole = second + first
    twice = cross + cross
    return apart * apart + twice * twice, whole * whole + 4096.0, cross, second + 64.0


def weighted(first, cross, second):
    spread, energy, cross, pivot = measures(first, cross, second)
    part = spread * recip(energy * pivot)
    return part * pivot + 0.1, part * cross


def join(weight_h, moment_h, first, cross, second):
    spread, energy, cross, pivot = measures(first, cross, second)
    above = moment_h * (energy * pivot) + spread * cross
    below = pivot * (energy * weight_h + spread)
    return -(above * recip(below))


def kernel(
    nv,
    nc,
    f_hbm,
    out,
    fv,
    full,
    got,
    wide,
    weight,
    moment,
    fix,
    slope,
    pack,
    pack_out,
    pack_l,
    pack_r,
    own_cols,
    cols_in,
    edge,
    edge_j,
    edge_d,
    load_sem,
    near_s,
    near_r,
    far_s,
    far_r,
    pack_s,
    pack_rs,
    cols_s,
    cols_r,
    ready,
):
    vi = lax.axis_index("views")
    cj = lax.axis_index("cols")
    odd = lax.rem(vi, 2)
    even = 1 - odd
    partner = vi + 1 - 2 * odd
    ahead = lax.rem(vi + nv + 2 - 4 * odd, nv)
    behind = lax.rem(vi + nv - 2 + 4 * odd, nv)
    left = lax.rem(cj + nc - 1, nc)
    right = lax.rem(cj + 1, nc)
    at_top = vi == 0
    at_bottom = vi == nv - 1
    has_far = jnp.logical_and(vi > 0, vi < nv - 1)
    sends_far = jnp.logical_and(vi != nv - 2, vi != 1)

    barrier = pltpu.get_barrier_semaphore()
    has_left, has_right = cj > 0, cj < nc - 1

    def greet(there):
        pl.semaphore_signal(barrier, inc=1, device_id=there, device_id_type=MESH)

    middle = nc // 2
    is_even = lax.rem(cj, 2) == 0
    late_l = jnp.logical_and(has_left, jnp.logical_and(is_even, cj != middle))
    late_r = jnp.logical_and(has_right, jnp.logical_or(is_even, cj == middle - 1))
    early_l = jnp.logical_and(has_left, jnp.logical_not(late_l))
    early_r = jnp.logical_and(has_right, jnp.logical_not(late_r))
    late_z = jnp.logical_and(has_far, odd == 0)
    early_z = jnp.logical_and(sends_far, odd == 0)
    late_q = jnp.logical_and(sends_far, odd == 1)
    early_q = jnp.logical_and(has_far, odd == 1)

    greet((partner, cj))
    for exists, there in (
        (early_z, (ahead, cj)),
        (early_q, (behind, cj)),
        (early_l, (vi, left)),
        (early_r, (vi, right)),
    ):

        @pl.when(exists)
        def _():
            greet(there)

    load = pltpu.make_async_copy(f_hbm, fv, load_sem)
    load.start()

    def remote(src, dst, s, r, there):
        return pltpu.make_async_remote_copy(
            src_ref=src, dst_ref=dst, send_sem=s, recv_sem=r, device_id=there, device_id_type=MESH
        )

    def near(k):
        span = pl.ds(k * CHUNK, CHUNK)
        return remote(f_hbm.at[:, span], got.at[odd, :, span], near_s, near_r.at[k], (partner, cj))

    def near_in(k):
        span = pl.ds(k * CHUNK, CHUNK)
        return remote(f_hbm.at[:, span], got.at[even, :, span], near_s, near_r.at[k], (partner, cj))

    def far(k):
        span = pl.ds(k * CHUNK, CHUNK)
        return remote(got.at[even, :, span], got.at[odd, :, span], far_s, far_r.at[k // 2], (ahead, cj))

    to_left = remote(pack_out.at[0], pack_r, pack_s.at[0], pack_rs.at[0], (vi, left))
    to_right = remote(pack_out.at[1], pack_l, pack_s.at[1], pack_rs.at[1], (vi, right))

    load.wait()

    row8 = lax.broadcasted_iota(jnp.int32, (8, PLANE), 0)
    row16 = lax.broadcasted_iota(jnp.int32, (16, X), 0)
    lane16 = lax.broadcasted_iota(jnp.int32, (16, X), 1)
    r8 = lax.rem(row16, 8)
    wanted = jnp.where(r8 < 4, r8 + (X - 4), r8 - 4)

    packed = jnp.zeros((16, PLANE), F32)
    for u in range(ROWS):
        pick = jnp.where(jnp.logical_and(lane16 == wanted, row16 // 8 == u), 1.0, 0.0).astype(BF16)
        packed = packed + lax.dot_general(
            pick, fv[u].reshape(PLANE, X), (((1,), (1,)), ((), ())), preferred_element_type=F32
        )
    pack[...] = packed.astype(BF16)

    def folded(a):
        return jnp.concatenate([a[:, : PLANE // 2], a[:, PLANE // 2 :]], axis=0).astype(BF16)

    def unfolded(a):
        a = a.astype(F32)
        return jnp.concatenate([a[:8], a[8:]], axis=1)

    pack_out[0] = folded(jnp.where(row8 < 4, pltpu.roll(packed[:8], 4, 0), packed[8:]))
    pack_out[1] = folded(jnp.where(row8 < 4, packed[:8], pltpu.roll(packed[8:], 4, 0)))
    four = jnp.where(row8 < 4, pltpu.roll(packed[:8], 6, 0), pltpu.roll(packed[8:], 2, 0))
    own_cols[...] = folded(four)

    greeted = jnp.int32(1)
    for late in (late_z, late_q, late_l, late_r):
        greeted = greeted + jnp.where(late, 1, 0)
    pl.semaphore_wait(barrier, greeted)

    def tell(which, there):
        pl.semaphore_signal(ready.at[which], inc=1, device_id=there, device_id_type=MESH)

    @pl.when(late_l)
    def _():
        to_left.start()
        tell(1, (vi, left))

    @pl.when(late_r)
    def _():
        to_right.start()
        tell(0, (vi, right))

    @pl.when(late_z)
    def _():
        tell(2, (behind, cj))

    cols_near = remote(own_cols, cols_in.at[1, odd], cols_s.at[0], cols_r.at[0], (partner, cj))
    cols_far = remote(cols_in.at[1, even], cols_in.at[1, odd], cols_s.at[1], cols_r.at[1], (ahead, cj))
    cols_near.start()
    for k in range(FIRST):
        near(k).start()

    held = jnp.logical_or(cj == nc // 2 - 1, cj == nc // 2)

    @pl.when(jnp.logical_not(held))
    def _():
        for k in range(FIRST, CHUNKS):
            near(k).start()

    def passed(far_too, slot):
        return (
            remote(
                cols_in.at[1, slot],
                cols_in.at[2, slot],
                cols_s.at[2 + far_too],
                cols_r.at[2 + far_too],
                (vi, left),
            ),
            remote(
                cols_in.at[1, slot],
                cols_in.at[0, slot],
                cols_s.at[4 + far_too],
                cols_r.at[4 + far_too],
                (vi, right),
            ),
        )

    near_left, near_right = passed(0, even)
    far_left, far_right = passed(1, odd)

    @pl.when(at_top)
    def _():
        got[0, 0] = fv[0]
        got[0, 1] = jnp.zeros((V, Y, X), BF16)

    @pl.when(at_bottom)
    def _():
        got[1, 0] = jnp.zeros((V, Y, X), BF16)
        got[1, 1] = fv[1]

    def lanes(a, k):
        return pltpu.roll(a, (-k) % a.shape[-1], a.ndim - 1)

    def smooth_lanes(a):
        pair = a + lanes(a, -1)
        return pair + lanes(pair, 1)

    def horizontal(i, carry):
        before, last = carry
        u = i // H_STEPS
        v0 = lax.rem(i, H_STEPS) * H_CHUNK
        top = v0 == 0
        before = [jnp.where(top, 0.0, c) for c in before]
        last = [jnp.where(top, 0.0, c) for c in last]
        here = fv[u, pl.ds(v0, H_CHUNK)].astype(F32)
        full[u, pl.ds(v0, H_CHUNK)] = here
        above = jnp.where(top, 0.0, fv[u, jnp.maximum(v0 - 1, 0)].astype(F32))
        below = jnp.where(
            v0 + H_CHUNK < V, fv[u, jnp.minimum(v0 + H_CHUNK, V - 1)].astype(F32), 0.0
        )
        mid_x = jnp.concatenate([above[None], here, below[None]], 0)
        left_x, right_x = lanes(mid_x, -1), lanes(mid_x, 1)
        grad_v = [a[2:] - a[:-2] for a in (left_x, mid_x, right_x)]
        grad_x = [here - lanes(here, -2), right_x[1:-1] - left_x[1:-1], lanes(here, 2) - here]

        def smooth_x(p, q):
            a, b, c = (s * t for s, t in zip(p, q))
            return (a + c) + (b + b)

        now = [smooth_x(grad_v, grad_v), smooth_x(grad_v, grad_x), smooth_x(grad_x, grad_x)]
        run = [jnp.concatenate([a[None], b[None], c], 0) for a, b, c in zip(before, last, now)]
        pairs = [c[1:] + c[:-1] for c in run]
        w, m = weighted(*(c[1:] + c[:-1] for c in pairs))
        weight[u, pl.ds(v0, H_CHUNK)] = w
        moment[u, pl.ds(v0, H_CHUNK)] = m

        @pl.when(v0 == V - H_CHUNK)
        def _():
            w, m = weighted(*(c[-1] + d[-1] for c, d in zip(pairs, now)))
            weight[u, V] = w
            moment[u, V] = m

        return [c[H_CHUNK - 2] for c in now], [c[H_CHUNK - 1] for c in now]

    zeros = [jnp.zeros((Y, X), F32)] * 3
    lax.fori_loop(0, 2 * H_STEPS, horizontal, (zeros, zeros))

    @pl.when(early_l)
    def _():
        pl.semaphore_wait(ready.at[0], 1)
        to_left.start()

    @pl.when(early_r)
    def _():
        pl.semaphore_wait(ready.at[1], 1)
        to_right.start()

    @pl.when(early_z)
    def _():
        pl.semaphore_wait(ready.at[2], 1)

    cols_near.wait_recv()

    @pl.when(sends_far)
    def _():
        cols_far.start()

    @pl.when(has_left)
    def _():
        near_left.start()

    @pl.when(has_right)
    def _():
        near_right.start()

    @pl.when(held)
    def _():
        for k in range(FIRST, SECOND):
            near(k).start()

    def relay(k):
        near_in(k).wait_recv()

        @pl.when(sends_far)
        def _():
            far(k).start()


    lane = lax.broadcasted_iota(jnp.int32, (STEP, 8, X), 2)
    sub = lax.broadcasted_iota(jnp.int32, (STEP, 8, X), 1)
    rim = jnp.logical_or(lane < 2, lane >= X - 2)
    outer = jnp.logical_or(lane == 0, lane == X - 1)

    def parts(ref, *at):
        return [ref[(*at, pl.ds(p, 8, stride=4), slice(None))] for p in range(4)]

    def y_up(a, rest=0.0):
        return a[1:] + [jnp.where(sub == 7, rest, pltpu.roll(a[0], 7, 1))]

    def y_down(a):
        return [jnp.where(sub == 0, 0.0, pltpu.roll(a[3], 1, 1))] + a[:3]

    def smooth_y(a):
        pair = [b + c for b, c in zip(a, y_down(a))]
        return [b + c for b, c in zip(pair, y_up(pair, a[3]))]

    def vertical(v0):
        span = pl.ds(v0, STEP)
        for slot in range(2):
            for u in range(ROWS):
                wide[2 * slot + u] = got[slot, u, span].astype(F32)
        every = slice(None)
        field = (
            [parts(wide, 0, every), parts(wide, 1, every)]
            + [parts(full, u, span) for u in range(ROWS)]
            + [parts(wide, 2, every), parts(wide, 3, every)]
        )
        comps = []
        for r in range(1, 5):
            grad_u = [a - b for a, b in zip(field[r + 1], field[r - 1])]
            grad_y = [a - b for a, b in zip(y_up(field[r]), y_down(field[r]))]
            comps.append(
                [
                    [a * b for a, b in zip(g, h)]
                    for g, h in ((grad_u, grad_u), (grad_u, grad_y), (grad_y, grad_y))
                ]
            )
        pairs = [
            [[a + b for a, b in zip(c, d)] for c, d in zip(comps[r], comps[r + 1])] for r in range(3)
        ]
        for u in range(ROWS):
            tensor = [
                smooth_y([a + b for a, b in zip(c, d)]) for c, d in zip(pairs[u], pairs[u + 1])
            ]
            past = pl.ds(v0 + 1, STEP)
            w, m = parts(weight, u, past), parts(moment, u, past)
            for p in range(4):
                slope[u, span, p] = join(w[p], m[p], *(c[p] for c in tensor))

    def variation(v0):
        span = pl.ds(v0, STEP)
        for u in range(ROWS):
            t = parts(fix, u, span)
            joined = [jnp.where(rim, t[p], slope[u, span, p]) for p in range(4)]
            flux_x, flux_y = [], []
            for here, below in zip(joined, y_up(joined)):
                step_x = lanes(here, 1) - here
                step_y = below - here
                scale = lax.rsqrt(step_x * step_x + step_y * step_y + 1.0)
                flux_x.append(step_x * scale)
                flux_y.append(step_y * scale)
            for p, above in enumerate(y_down(flux_y)):
                depth = joined[p] + 0.2 * (flux_x[p] - lanes(flux_x[p], -1) + flux_y[p] - above)
                out[u, span, pl.ds(p, 8, stride=4), :] = jnp.where(outer, lanes(t[p], -63), depth)

    place = lax.broadcasted_iota(jnp.int32, (8, PLANE), 1)
    y_at = lax.rem(place, Y)

    def cols_by(a, k):
        return pltpu.roll(a, (-k) % 8, 0)

    def y_by(a, k):
        return jnp.where(y_at == (Y - 1 if k > 0 else 0), 0.0, pltpu.roll(a, (-k) % PLANE, 1))

    def v_by(a, k):
        return jnp.where(
            place >= PLANE - Y if k > 0 else place < Y, 0.0, pltpu.roll(a, (-k * Y) % PLANE, 1)
        )

    def smooth_by(by, a):
        return by(a, -1) + (a + a) + by(a, 1)

    for k in range(4):
        relay(k)

    @pl.when(has_far)
    def _():
        cols_far.wait_recv()

        @pl.when(has_left)
        def _():
            far_left.start()

        @pl.when(has_right)
        def _():
            far_right.start()

    @pl.when(held)
    def _():
        for k in range(SECOND, CHUNKS):
            near(k).start()

    relay(4)
    @pl.when(has_left)
    def _():
        to_right.wait_recv()

    @pl.when(has_right)
    def _():
        to_left.wait_recv()

    first, final = cj == 0, cj == nc - 1
    own = pack[...].astype(F32)
    from_l = unfolded(pack_l[...])
    from_r = unfolded(pack_r[...])
    for u in range(ROWS):
        mine = own[8 * u : 8 * u + 8]
        l_in = pltpu.roll(from_l, 4, 0) if u else from_l
        r_in = from_r if u else pltpu.roll(from_r, 4, 0)
        flip_l = jnp.where(row8 == 2, pltpu.roll(mine, 6, 0), 0.0)
        flip_r = jnp.where(row8 == 5, pltpu.roll(mine, 2, 0), 0.0)
        l_in = jnp.where(first, flip_l, l_in)
        r_in = jnp.where(final, flip_r, r_in)
        e_l = jnp.where(row8 < 4, l_in, mine)
        e_r = jnp.where(row8 < 4, mine, r_in)
        edge[0, 2 + u] = e_l
        edge[1, 2 + u] = e_r

    def edges_h(side, carry):
        for u in range(ROWS):
            f = edge[side, 2 + u]
            grad_v = v_by(f, 1) - v_by(f, -1)
            grad_x = cols_by(f, 1) - cols_by(f, -1)
            w, m = weighted(
                *(
                    smooth_by(v_by, smooth_by(cols_by, c))
                    for c in (grad_v * grad_v, grad_v * grad_x, grad_x * grad_x)
                )
            )
            edge_j[side, u] = w
            edge_d[side, u] = m
        relay(5 + side)
        return carry

    lax.fori_loop(0, 2, edges_h, 0)


    def arrived(g):
        @pl.when(has_far)
        def _():
            both = pl.ds(g * STEP, STEP)
            remote(
                got.at[even, :, both], got.at[odd, :, both], far_s, far_r.at[g], (ahead, cj)
            ).wait_recv()

    def start(g, carry):
        @pl.when(g > 0)
        def _():
            relay(2 * g + 6)

        relay(2 * g + 7)
        arrived(g)
        vertical(g * STEP)
        return carry

    lax.fori_loop(0, BEFORE, start, 0)

    @pl.when(has_left)
    def _():
        near_right.wait_recv()

        @pl.when(has_far)
        def _():
            far_right.wait_recv()

    @pl.when(has_right)
    def _():
        near_left.wait_recv()

        @pl.when(has_far)
        def _():
            far_left.wait_recv()

    for slot in range(2):
        from_l, here, from_r = (
            unfolded(cols_in[origin, slot]) for origin in range(3)
        )
        for u in range(ROWS):
            with_l = jnp.where(row8 == 4 * u + 1, from_l, here)
            with_r = jnp.where(row8 == 4 * u + 2, from_r, here)
            edge[0, 4 * slot + u] = pltpu.roll(with_l, 2 + 4 * u, 0)
            edge[1, 4 * slot + u] = pltpu.roll(with_r, 2 + 4 * u, 0)

    @pl.when(at_top)
    def _():
        for side in range(2):
            edge[side, 0] = edge[side, 2]
            edge[side, 1] = jnp.zeros((8, PLANE), F32)

    @pl.when(at_bottom)
    def _():
        for side in range(2):
            edge[side, 4] = jnp.zeros((8, PLANE), F32)
            edge[side, 5] = edge[side, 3]

    def edges(side, carry):
        relay(2 * BEFORE + 6 + side)
        j_below = jnp.where(jnp.logical_and(final, side == 1), 4, 8)
        q_from = jnp.where(jnp.logical_and(first, side == 0), 4, 0)
        tiles = [edge[side, r] for r in range(6)]
        comps = []
        for r in range(1, 5):
            grad_u = tiles[r + 1] - tiles[r - 1]
            grad_y = y_by(tiles[r], 1) - y_by(tiles[r], -1)
            comps.append((grad_u * grad_u, grad_u * grad_y, grad_y * grad_y))
        for u in range(ROWS):
            w, m = edge_j[side, u], edge_d[side, u]
            tensor = [
                smooth_by(y_by, a + (b + b) + c) for a, b, c in zip(comps[u], comps[u + 1], comps[u + 2])
            ]
            joined = jnp.where(row8 < j_below, join(w, m, *tensor), 0.0)
            step_x = cols_by(joined, 1) - joined
            step_y = y_by(joined, 1) - joined
            scale = lax.rsqrt(step_x * step_x + step_y * step_y + 1.0)
            flux_x = jnp.where(row8 >= q_from, step_x * scale, 0.0)
            flux_y = step_y * scale
            depth = joined + 0.2 * (flux_x - cols_by(flux_x, -1) + flux_y - y_by(flux_y, -1))
            edge_j[side, u] = pltpu.roll(joined, 4, 0)
            edge_d[side, u] = pltpu.roll(depth, 5, 0)
        return carry

    lax.fori_loop(0, 2, edges, 0)

    small = lax.broadcasted_iota(jnp.int32, (8, X), 0)

    def spread_out(u, carry):
        for b in range(PLANE // X):
            part = pl.ds(b * X, X)
            both = jnp.where(small == 0, edge_d[1, u, :, part], edge_d[0, u, :, part])
            block = jnp.concatenate(
                [
                    edge_j[0, u, :, part],
                    jnp.zeros((56, X), F32),
                    both,
                    jnp.zeros((48, X), F32),
                    edge_j[1, u, :, part],
                ],
                axis=0,
            )
            fix[u, pl.ds(4 * b, 4)] = block.T.reshape(4, Y, X)
        return carry

    relay(2 * BEFORE + 8)
    lax.fori_loop(0, 2, spread_out, 0)

    def finish(g, carry):
        for k in range(2):

            @pl.when(2 * g + k + 9 < CHUNKS)
            def _():
                relay(2 * g + k + 9)

        def varied(i, c):
            variation(i * STEP)
            return c

        lax.fori_loop(jnp.where(g == BEFORE, 0, g - 1), g, varied, 0)
        arrived(g)
        vertical(g * STEP)
        return carry

    lax.fori_loop(BEFORE, V // STEP, finish, 0)
    variation(V - STEP)

    @pl.when(has_left)
    def _():
        to_left.wait_send()
        near_left.wait_send()

    @pl.when(has_right)
    def _():
        to_right.wait_send()
        near_right.wait_send()

    @pl.when(jnp.logical_and(has_left, has_far))
    def _():
        far_left.wait_send()

    @pl.when(jnp.logical_and(has_right, has_far))
    def _():
        far_right.wait_send()

    cols_near.wait_send()
    remote(f_hbm, got.at[odd], near_s, near_r.at[0], (partner, cj)).wait_send()

    @pl.when(sends_far)
    def _():
        cols_far.wait_send()
        remote(got.at[even], got.at[odd], far_s, far_r.at[0], (ahead, cj)).wait_send()


def local(nv, nc, light_field):
    block = (ROWS, V, Y, X)
    dma = pltpu.SemaphoreType.DMA
    return pl.pallas_call(
        functools.partial(kernel, nv, nc),
        out_shape=jax.ShapeDtypeStruct(block, F32),
        in_specs=[pl.BlockSpec(memory_space=pl.ANY)],
        out_specs=pl.BlockSpec(memory_space=pltpu.VMEM),
        scratch_shapes=[
            pltpu.VMEM(block, BF16),
            pltpu.VMEM(block, F32),
            pltpu.VMEM((2, *block), BF16),
            pltpu.VMEM((4, STEP, Y, X), F32),
            pltpu.VMEM((ROWS, V + 1, Y, X), F32),
            pltpu.VMEM((ROWS, V + 1, Y, X), F32),
            pltpu.VMEM(block, F32),
            pltpu.VMEM((ROWS, V, 4, 8, X), F32),
            pltpu.VMEM((16, PLANE), BF16),
            pltpu.VMEM((2, 16, PLANE // 2), BF16),
            pltpu.VMEM((16, PLANE // 2), BF16),
            pltpu.VMEM((16, PLANE // 2), BF16),
            pltpu.VMEM((16, PLANE // 2), BF16),
            pltpu.VMEM((3, 2, 16, PLANE // 2), BF16),
            pltpu.VMEM((2, 6, 8, PLANE), F32),
            pltpu.VMEM((2, ROWS, 8, PLANE), F32),
            pltpu.VMEM((2, ROWS, 8, PLANE), F32),
            dma,
            dma,
            dma((CHUNKS,)),
            dma,
            dma((CHUNKS // 2,)),
            dma((2,)),
            dma((2,)),
            dma((6,)),
            dma((6,)),
            pltpu.SemaphoreType.REGULAR((3,)),
        ],
        compiler_params=pltpu.CompilerParams(
            collective_id=0, has_side_effects=True, vmem_limit_bytes=32 << 20
        ),
        cost_estimate=pl.CostEstimate(flops=60_000_000, bytes_accessed=1_600_000, transcendentals=800_000),
    )(pltpu.with_memory_space_constraint(light_field, pltpu.HBM))


def solution(mesh):
    return jax.shard_map(
        functools.partial(local, mesh.shape["views"], mesh.shape["cols"]),
        mesh=mesh,
        in_specs=(P("views", None, None, "cols"),),
        out_specs=P("views", None, None, "cols"),
        check_vma=False,
    )
```

```python
import functools

import jax
import jax.numpy as jnp
from jax import lax
from jax.experimental import pallas as pl
from jax.experimental.pallas import tpu as pltpu
from jax.sharding import PartitionSpec as P

MESH = pl.DeviceIdType.MESH
F32 = jnp.float32
BF16 = jnp.bfloat16
ROWS, V, Y, X = 2, 32, 32, 128
CHUNK = 2
CHUNKS = V // CHUNK
STEP = 4
H_CHUNK = 8
H_STEPS = V // H_CHUNK
BEFORE = 3
FIRST = 6
SECOND = 11
PLANE = V * Y


def recip(x):
    r = pl.reciprocal(x, approx=True)
    return r * (2.0 - x * r)


def measures(first, cross, second):
    apart = second - first
    whole = second + first
    twice = cross + cross
    return apart * apart + twice * twice, whole * whole + 4096.0, cross, second + 64.0


def weighted(first, cross, second):
    spread, energy, cross, pivot = measures(first, cross, second)
    part = spread * recip(energy * pivot)
    return part * pivot + 0.1, part * cross


def join(weight_h, moment_h, first, cross, second):
    spread, energy, cross, pivot = measures(first, cross, second)
    above = moment_h * (energy * pivot) + spread * cross
    below = pivot * (energy * weight_h + spread)
    return -(above * recip(below))


def kernel(
    nv,
    nc,
    f_hbm,
    out,
    fv,
    full,
    got,
    wide,
    weight,
    moment,
    fix,
    slope,
    pack,
    pack_out,
    pack_l,
    pack_r,
    own_cols,
    cols_in,
    edge,
    edge_j,
    edge_d,
    load_sem,
    near_s,
    near_r,
    far_s,
    far_r,
    pack_s,
    pack_rs,
    cols_s,
    cols_r,
    ready,
):
    vi = lax.axis_index("views")
    cj = lax.axis_index("cols")
    odd = lax.rem(vi, 2)
    even = 1 - odd
    partner = vi + 1 - 2 * odd
    ahead = lax.rem(vi + nv + 2 - 4 * odd, nv)
    behind = lax.rem(vi + nv - 2 + 4 * odd, nv)
    left = lax.rem(cj + nc - 1, nc)
    right = lax.rem(cj + 1, nc)
    at_top = vi == 0
    at_bottom = vi == nv - 1
    has_far = jnp.logical_and(vi > 0, vi < nv - 1)
    sends_far = jnp.logical_and(vi != nv - 2, vi != 1)

    barrier = pltpu.get_barrier_semaphore()
    has_left, has_right = cj > 0, cj < nc - 1

    def greet(there):
        pl.semaphore_signal(barrier, inc=1, device_id=there, device_id_type=MESH)

    middle = nc // 2
    is_even = lax.rem(cj, 2) == 0
    late_l = jnp.logical_and(has_left, jnp.logical_and(is_even, cj != middle))
    late_r = jnp.logical_and(has_right, jnp.logical_or(is_even, cj == middle - 1))
    early_l = jnp.logical_and(has_left, jnp.logical_not(late_l))
    early_r = jnp.logical_and(has_right, jnp.logical_not(late_r))
    late_z = jnp.logical_and(has_far, odd == 0)
    early_z = jnp.logical_and(sends_far, odd == 0)
    late_q = jnp.logical_and(sends_far, odd == 1)
    early_q = jnp.logical_and(has_far, odd == 1)

    greet((partner, cj))
    for exists, there in (
        (early_z, (ahead, cj)),
        (early_q, (behind, cj)),
        (early_l, (vi, left)),
        (early_r, (vi, right)),
    ):

        @pl.when(exists)
        def _():
            greet(there)

    load = pltpu.make_async_copy(f_hbm, fv, load_sem)
    load.start()

    def remote(src, dst, s, r, there):
        return pltpu.make_async_remote_copy(
            src_ref=src, dst_ref=dst, send_sem=s, recv_sem=r, device_id=there, device_id_type=MESH
        )

    def near(k):
        span = pl.ds(k * CHUNK, CHUNK)
        return remote(f_hbm.at[:, span], got.at[odd, :, span], near_s, near_r.at[k], (partner, cj))

    def near_in(k):
        span = pl.ds(k * CHUNK, CHUNK)
        return remote(f_hbm.at[:, span], got.at[even, :, span], near_s, near_r.at[k], (partner, cj))

    def far(k):
        span = pl.ds(k * CHUNK, CHUNK)
        return remote(got.at[even, :, span], got.at[odd, :, span], far_s, far_r.at[k // 2], (ahead, cj))

    to_left = remote(pack_out.at[0], pack_r, pack_s.at[0], pack_rs.at[0], (vi, left))
    to_right = remote(pack_out.at[1], pack_l, pack_s.at[1], pack_rs.at[1], (vi, right))

    load.wait()

    row8 = lax.broadcasted_iota(jnp.int32, (8, PLANE), 0)
    row16 = lax.broadcasted_iota(jnp.int32, (16, X), 0)
    lane16 = lax.broadcasted_iota(jnp.int32, (16, X), 1)
    r8 = lax.rem(row16, 8)
    wanted = jnp.where(r8 < 4, r8 + (X - 4), r8 - 4)

    packed = jnp.zeros((16, PLANE), F32)
    for u in range(ROWS):
        pick = jnp.where(jnp.logical_and(lane16 == wanted, row16 // 8 == u), 1.0, 0.0).astype(BF16)
        packed = packed + lax.dot_general(
            pick, fv[u].reshape(PLANE, X), (((1,), (1,)), ((), ())), preferred_element_type=F32
        )
    pack[...] = packed.astype(BF16)

    def folded(a):
        return jnp.concatenate([a[:, : PLANE // 2], a[:, PLANE // 2 :]], axis=0).astype(BF16)

    def unfolded(a):
        a = a.astype(F32)
        return jnp.concatenate([a[:8], a[8:]], axis=1)

    pack_out[0] = folded(jnp.where(row8 < 4, pltpu.roll(packed[:8], 4, 0), packed[8:]))
    pack_out[1] = folded(jnp.where(row8 < 4, packed[:8], pltpu.roll(packed[8:], 4, 0)))
    four = jnp.where(row8 < 4, pltpu.roll(packed[:8], 6, 0), pltpu.roll(packed[8:], 2, 0))
    own_cols[...] = folded(four)

    greeted = jnp.int32(1)
    for late in (late_z, late_q, late_l, late_r):
        greeted = greeted + jnp.where(late, 1, 0)
    pl.semaphore_wait(barrier, greeted)

    def tell(which, there):
        pl.semaphore_signal(ready.at[which], inc=1, device_id=there, device_id_type=MESH)

    @pl.when(late_l)
    def _():
        to_left.start()
        tell(1, (vi, left))

    @pl.when(late_r)
    def _():
        to_right.start()
        tell(0, (vi, right))

    @pl.when(late_z)
    def _():
        tell(2, (behind, cj))

    cols_near = remote(own_cols, cols_in.at[1, odd], cols_s.at[0], cols_r.at[0], (partner, cj))
    cols_far = remote(cols_in.at[1, even], cols_in.at[1, odd], cols_s.at[1], cols_r.at[1], (ahead, cj))
    cols_near.start()
    for k in range(FIRST):
        near(k).start()

    held = jnp.logical_or(cj == nc // 2 - 1, cj == nc // 2)

    @pl.when(jnp.logical_not(held))
    def _():
        for k in range(FIRST, CHUNKS):
            near(k).start()

    def passed(far_too, slot):
        return (
            remote(
                cols_in.at[1, slot],
                cols_in.at[2, slot],
                cols_s.at[2 + far_too],
                cols_r.at[2 + far_too],
                (vi, left),
            ),
            remote(
                cols_in.at[1, slot],
                cols_in.at[0, slot],
                cols_s.at[4 + far_too],
                cols_r.at[4 + far_too],
                (vi, right),
            ),
        )

    near_left, near_right = passed(0, even)
    far_left, far_right = passed(1, odd)

    @pl.when(at_top)
    def _():
        got[0, 0] = fv[0]
        got[0, 1] = jnp.zeros((V, Y, X), BF16)

    @pl.when(at_bottom)
    def _():
        got[1, 0] = jnp.zeros((V, Y, X), BF16)
        got[1, 1] = fv[1]

    def lanes(a, k):
        return pltpu.roll(a, (-k) % a.shape[-1], a.ndim - 1)

    def smooth_lanes(a):
        pair = a + lanes(a, -1)
        return pair + lanes(pair, 1)

    def horizontal(i, carry):
        before, last = carry
        u = i // H_STEPS
        v0 = lax.rem(i, H_STEPS) * H_CHUNK
        top = v0 == 0
        before = [jnp.where(top, 0.0, c) for c in before]
        last = [jnp.where(top, 0.0, c) for c in last]
        here = fv[u, pl.ds(v0, H_CHUNK)].astype(F32)
        full[u, pl.ds(v0, H_CHUNK)] = here
        above = jnp.where(top, 0.0, fv[u, jnp.maximum(v0 - 1, 0)].astype(F32))
        below = jnp.where(
            v0 + H_CHUNK < V, fv[u, jnp.minimum(v0 + H_CHUNK, V - 1)].astype(F32), 0.0
        )
        mid_x = jnp.concatenate([above[None], here, below[None]], 0)
        left_x, right_x = lanes(mid_x, -1), lanes(mid_x, 1)
        grad_v = [a[2:] - a[:-2] for a in (left_x, mid_x, right_x)]
        grad_x = [here - lanes(here, -2), right_x[1:-1] - left_x[1:-1], lanes(here, 2) - here]

        def smooth_x(p, q):
            a, b, c = (s * t for s, t in zip(p, q))
            return (a + c) + (b + b)

        now = [smooth_x(grad_v, grad_v), smooth_x(grad_v, grad_x), smooth_x(grad_x, grad_x)]
        run = [jnp.concatenate([a[None], b[None], c], 0) for a, b, c in zip(before, last, now)]
        pairs = [c[1:] + c[:-1] for c in run]
        w, m = weighted(*(c[1:] + c[:-1] for c in pairs))
        weight[u, pl.ds(v0, H_CHUNK)] = w
        moment[u, pl.ds(v0, H_CHUNK)] = m

        @pl.when(v0 == V - H_CHUNK)
        def _():
            w, m = weighted(*(c[-1] + d[-1] for c, d in zip(pairs, now)))
            weight[u, V] = w
            moment[u, V] = m

        return [c[H_CHUNK - 2] for c in now], [c[H_CHUNK - 1] for c in now]

    zeros = [jnp.zeros((Y, X), F32)] * 3
    lax.fori_loop(0, 2 * H_STEPS, horizontal, (zeros, zeros))

    @pl.when(early_l)
    def _():
        pl.semaphore_wait(ready.at[0], 1)
        to_left.start()

    @pl.when(early_r)
    def _():
        pl.semaphore_wait(ready.at[1], 1)
        to_right.start()

    @pl.when(early_z)
    def _():
        pl.semaphore_wait(ready.at[2], 1)

    cols_near.wait_recv()

    @pl.when(sends_far)
    def _():
        cols_far.start()

    @pl.when(has_left)
    def _():
        near_left.start()

    @pl.when(has_right)
    def _():
        near_right.start()

    @pl.when(held)
    def _():
        for k in range(FIRST, SECOND):
            near(k).start()

    def relay(k):
        near_in(k).wait_recv()

        @pl.when(sends_far)
        def _():
            far(k).start()


    lane = lax.broadcasted_iota(jnp.int32, (STEP, Y, X), 2)
    sub = lax.broadcasted_iota(jnp.int32, (STEP, Y, X), 1)
    rim = jnp.logical_or(lane < 2, lane >= X - 2)
    outer = jnp.logical_or(lane == 0, lane == X - 1)

    def parts(ref, *at):
        return [ref[at]]

    def y_up(a, rest=0.0):
        return [jnp.where(sub == Y - 1, rest, pltpu.roll(a[0], Y - 1, 1))]

    def y_down(a):
        return [jnp.where(sub == 0, 0.0, pltpu.roll(a[0], 1, 1))]

    def smooth_y(a):
        pair = [b + c for b, c in zip(a, y_down(a))]
        return [b + c for b, c in zip(pair, y_up(pair, a[0]))]

    def vertical(v0):
        span = pl.ds(v0, STEP)
        for slot in range(2):
            for u in range(ROWS):
                wide[2 * slot + u] = got[slot, u, span].astype(F32)
        every = slice(None)
        field = (
            [parts(wide, 0, every), parts(wide, 1, every)]
            + [parts(full, u, span) for u in range(ROWS)]
            + [parts(wide, 2, every), parts(wide, 3, every)]
        )
        comps = []
        for r in range(1, 5):
            grad_u = [a - b for a, b in zip(field[r + 1], field[r - 1])]
            grad_y = [a - b for a, b in zip(y_up(field[r]), y_down(field[r]))]
            comps.append(
                [
                    [a * b for a, b in zip(g, h)]
                    for g, h in ((grad_u, grad_u), (grad_u, grad_y), (grad_y, grad_y))
                ]
            )
        pairs = [
            [[a + b for a, b in zip(c, d)] for c, d in zip(comps[r], comps[r + 1])] for r in range(3)
        ]
        for u in range(ROWS):
            tensor = [
                smooth_y([a + b for a, b in zip(c, d)]) for c, d in zip(pairs[u], pairs[u + 1])
            ]
            past = pl.ds(v0 + 1, STEP)
            w, m = parts(weight, u, past), parts(moment, u, past)
            slope[u, span] = join(w[0], m[0], *(c[0] for c in tensor))

    def variation(v0):
        span = pl.ds(v0, STEP)
        for u in range(ROWS):
            t = parts(fix, u, span)
            joined = [jnp.where(rim, t[0], slope[u, span])]
            flux_x, flux_y = [], []
            for here, below in zip(joined, y_up(joined)):
                step_x = lanes(here, 1) - here
                step_y = below - here
                scale = lax.rsqrt(step_x * step_x + step_y * step_y + 1.0)
                flux_x.append(step_x * scale)
                flux_y.append(step_y * scale)
            for p, above in enumerate(y_down(flux_y)):
                depth = joined[p] + 0.2 * (flux_x[p] - lanes(flux_x[p], -1) + flux_y[p] - above)
                out[u, span] = jnp.where(outer, lanes(t[p], -63), depth)

    place = lax.broadcasted_iota(jnp.int32, (8, PLANE), 1)
    y_at = lax.rem(place, Y)

    def cols_by(a, k):
        return pltpu.roll(a, (-k) % 8, 0)

    def y_by(a, k):
        return jnp.where(y_at == (Y - 1 if k > 0 else 0), 0.0, pltpu.roll(a, (-k) % PLANE, 1))

    def v_by(a, k):
        return jnp.where(
            place >= PLANE - Y if k > 0 else place < Y, 0.0, pltpu.roll(a, (-k * Y) % PLANE, 1)
        )

    def smooth_by(by, a):
        return by(a, -1) + (a + a) + by(a, 1)

    for k in range(4):
        relay(k)

    @pl.when(has_far)
    def _():
        cols_far.wait_recv()

        @pl.when(has_left)
        def _():
            far_left.start()

        @pl.when(has_right)
        def _():
            far_right.start()

    @pl.when(held)
    def _():
        for k in range(SECOND, CHUNKS):
            near(k).start()

    relay(4)
    @pl.when(has_left)
    def _():
        to_right.wait_recv()

    @pl.when(has_right)
    def _():
        to_left.wait_recv()

    first, final = cj == 0, cj == nc - 1
    own = pack[...].astype(F32)
    from_l = unfolded(pack_l[...])
    from_r = unfolded(pack_r[...])
    for u in range(ROWS):
        mine = own[8 * u : 8 * u + 8]
        l_in = pltpu.roll(from_l, 4, 0) if u else from_l
        r_in = from_r if u else pltpu.roll(from_r, 4, 0)
        flip_l = jnp.where(row8 == 2, pltpu.roll(mine, 6, 0), 0.0)
        flip_r = jnp.where(row8 == 5, pltpu.roll(mine, 2, 0), 0.0)
        l_in = jnp.where(first, flip_l, l_in)
        r_in = jnp.where(final, flip_r, r_in)
        e_l = jnp.where(row8 < 4, l_in, mine)
        e_r = jnp.where(row8 < 4, mine, r_in)
        edge[0, 2 + u] = e_l
        edge[1, 2 + u] = e_r

    def edges_h(side, carry):
        for u in range(ROWS):
            f = edge[side, 2 + u]
            grad_v = v_by(f, 1) - v_by(f, -1)
            grad_x = cols_by(f, 1) - cols_by(f, -1)
            w, m = weighted(
                *(
                    smooth_by(v_by, smooth_by(cols_by, c))
                    for c in (grad_v * grad_v, grad_v * grad_x, grad_x * grad_x)
                )
            )
            edge_j[side, u] = w
            edge_d[side, u] = m
        relay(5 + side)
        return carry

    lax.fori_loop(0, 2, edges_h, 0)


    def arrived(g):
        @pl.when(has_far)
        def _():
            both = pl.ds(g * STEP, STEP)
            remote(
                got.at[even, :, both], got.at[odd, :, both], far_s, far_r.at[g], (ahead, cj)
            ).wait_recv()

    def start(g, carry):
        @pl.when(g > 0)
        def _():
            relay(2 * g + 6)

        relay(2 * g + 7)
        arrived(g)
        vertical(g * STEP)
        return carry

    lax.fori_loop(0, BEFORE, start, 0)

    @pl.when(has_left)
    def _():
        near_right.wait_recv()

        @pl.when(has_far)
        def _():
            far_right.wait_recv()

    @pl.when(has_right)
    def _():
        near_left.wait_recv()

        @pl.when(has_far)
        def _():
            far_left.wait_recv()

    for slot in range(2):
        from_l, here, from_r = (
            unfolded(cols_in[origin, slot]) for origin in range(3)
        )
        for u in range(ROWS):
            with_l = jnp.where(row8 == 4 * u + 1, from_l, here)
            with_r = jnp.where(row8 == 4 * u + 2, from_r, here)
            edge[0, 4 * slot + u] = pltpu.roll(with_l, 2 + 4 * u, 0)
            edge[1, 4 * slot + u] = pltpu.roll(with_r, 2 + 4 * u, 0)

    @pl.when(at_top)
    def _():
        for side in range(2):
            edge[side, 0] = edge[side, 2]
            edge[side, 1] = jnp.zeros((8, PLANE), F32)

    @pl.when(at_bottom)
    def _():
        for side in range(2):
            edge[side, 4] = jnp.zeros((8, PLANE), F32)
            edge[side, 5] = edge[side, 3]

    def edges(side, carry):
        relay(2 * BEFORE + 6 + side)
        j_below = jnp.where(jnp.logical_and(final, side == 1), 4, 8)
        q_from = jnp.where(jnp.logical_and(first, side == 0), 4, 0)
        tiles = [edge[side, r] for r in range(6)]
        comps = []
        for r in range(1, 5):
            grad_u = tiles[r + 1] - tiles[r - 1]
            grad_y = y_by(tiles[r], 1) - y_by(tiles[r], -1)
            comps.append((grad_u * grad_u, grad_u * grad_y, grad_y * grad_y))
        for u in range(ROWS):
            w, m = edge_j[side, u], edge_d[side, u]
            tensor = [
                smooth_by(y_by, a + (b + b) + c) for a, b, c in zip(comps[u], comps[u + 1], comps[u + 2])
            ]
            joined = jnp.where(row8 < j_below, join(w, m, *tensor), 0.0)
            step_x = cols_by(joined, 1) - joined
            step_y = y_by(joined, 1) - joined
            scale = lax.rsqrt(step_x * step_x + step_y * step_y + 1.0)
            flux_x = jnp.where(row8 >= q_from, step_x * scale, 0.0)
            flux_y = step_y * scale
            depth = joined + 0.2 * (flux_x - cols_by(flux_x, -1) + flux_y - y_by(flux_y, -1))
            edge_j[side, u] = pltpu.roll(joined, 4, 0)
            edge_d[side, u] = pltpu.roll(depth, 5, 0)
        return carry

    lax.fori_loop(0, 2, edges, 0)

    small = lax.broadcasted_iota(jnp.int32, (8, X), 0)

    def spread_out(u, carry):
        for b in range(PLANE // X):
            part = pl.ds(b * X, X)
            both = jnp.where(small == 0, edge_d[1, u, :, part], edge_d[0, u, :, part])
            block = jnp.concatenate(
                [
                    edge_j[0, u, :, part],
                    jnp.zeros((56, X), F32),
                    both,
                    jnp.zeros((48, X), F32),
                    edge_j[1, u, :, part],
                ],
                axis=0,
            )
            fix[u, pl.ds(4 * b, 4)] = block.T.reshape(4, Y, X)
        return carry

    relay(2 * BEFORE + 8)
    lax.fori_loop(0, 2, spread_out, 0)

    def finish(g, carry):
        for k in range(2):

            @pl.when(2 * g + k + 9 < CHUNKS)
            def _():
                relay(2 * g + k + 9)

        def varied(i, c):
            variation(i * STEP)
            return c

        lax.fori_loop(jnp.where(g == BEFORE, 0, g - 1), g, varied, 0)
        arrived(g)
        vertical(g * STEP)
        return carry

    lax.fori_loop(BEFORE, V // STEP, finish, 0)
    variation(V - STEP)

    @pl.when(has_left)
    def _():
        to_left.wait_send()
        near_left.wait_send()

    @pl.when(has_right)
    def _():
        to_right.wait_send()
        near_right.wait_send()

    @pl.when(jnp.logical_and(has_left, has_far))
    def _():
        far_left.wait_send()

    @pl.when(jnp.logical_and(has_right, has_far))
    def _():
        far_right.wait_send()

    cols_near.wait_send()
    remote(f_hbm, got.at[odd], near_s, near_r.at[0], (partner, cj)).wait_send()

    @pl.when(sends_far)
    def _():
        cols_far.wait_send()
        remote(got.at[even], got.at[odd], far_s, far_r.at[0], (ahead, cj)).wait_send()


def local(nv, nc, light_field):
    block = (ROWS, V, Y, X)
    dma = pltpu.SemaphoreType.DMA
    return pl.pallas_call(
        functools.partial(kernel, nv, nc),
        out_shape=jax.ShapeDtypeStruct(block, F32),
        in_specs=[pl.BlockSpec(memory_space=pl.ANY)],
        out_specs=pl.BlockSpec(memory_space=pltpu.VMEM),
        scratch_shapes=[
            pltpu.VMEM(block, BF16),
            pltpu.VMEM(block, F32),
            pltpu.VMEM((2, *block), BF16),
            pltpu.VMEM((4, STEP, Y, X), F32),
            pltpu.VMEM((ROWS, V + 1, Y, X), F32),
            pltpu.VMEM((ROWS, V + 1, Y, X), F32),
            pltpu.VMEM(block, F32),
            pltpu.VMEM(block, F32),
            pltpu.VMEM((16, PLANE), BF16),
            pltpu.VMEM((2, 16, PLANE // 2), BF16),
            pltpu.VMEM((16, PLANE // 2), BF16),
            pltpu.VMEM((16, PLANE // 2), BF16),
            pltpu.VMEM((16, PLANE // 2), BF16),
            pltpu.VMEM((3, 2, 16, PLANE // 2), BF16),
            pltpu.VMEM((2, 6, 8, PLANE), F32),
            pltpu.VMEM((2, ROWS, 8, PLANE), F32),
            pltpu.VMEM((2, ROWS, 8, PLANE), F32),
            dma,
            dma,
            dma((CHUNKS,)),
            dma,
            dma((CHUNKS // 2,)),
            dma((2,)),
            dma((2,)),
            dma((6,)),
            dma((6,)),
            pltpu.SemaphoreType.REGULAR((3,)),
        ],
        compiler_params=pltpu.CompilerParams(
            collective_id=0, has_side_effects=True, vmem_limit_bytes=32 << 20
        ),
        cost_estimate=pl.CostEstimate(flops=60_000_000, bytes_accessed=1_600_000, transcendentals=800_000),
    )(pltpu.with_memory_space_constraint(light_field, pltpu.HBM))


def solution(mesh):
    return jax.shard_map(
        functools.partial(local, mesh.shape["views"], mesh.shape["cols"]),
        mesh=mesh,
        in_specs=(P("views", None, None, "cols"),),
        out_specs=P("views", None, None, "cols"),
        check_vma=False,
    )
```

```python
import functools

import jax
import jax.numpy as jnp
from jax import lax
from jax.experimental import pallas as pl
from jax.experimental.pallas import tpu as pltpu
from jax.sharding import PartitionSpec as P

MESH = pl.DeviceIdType.MESH
F32 = jnp.float32
BF16 = jnp.bfloat16
ROWS, V, Y, X = 2, 32, 32, 128
CHUNK = 2
CHUNKS = V // CHUNK
STEP = 4
H_CHUNK = 8
H_STEPS = V // H_CHUNK
BEFORE = 3
FIRST = 5
SECOND = 12
PLANE = V * Y


def recip(x):
    r = pl.reciprocal(x, approx=True)
    return r * (2.0 - x * r)


def measures(first, cross, second):
    apart = second - first
    whole = second + first
    twice = cross + cross
    return apart * apart + twice * twice, whole * whole + 4096.0, cross, second + 64.0


def weighted(first, cross, second):
    spread, energy, cross, pivot = measures(first, cross, second)
    part = spread * recip(energy * pivot)
    return part * pivot + 0.1, part * cross


def join(weight_h, moment_h, first, cross, second):
    spread, energy, cross, pivot = measures(first, cross, second)
    above = moment_h * (energy * pivot) + spread * cross
    below = pivot * (energy * weight_h + spread)
    return -(above * recip(below))


def kernel(
    nv,
    nc,
    f_hbm,
    out,
    fv,
    full,
    got,
    wide,
    weight,
    moment,
    fix,
    slope,
    pack,
    pack_out,
    pack_l,
    pack_r,
    own_cols,
    cols_in,
    edge,
    edge_j,
    edge_d,
    load_sem,
    near_s,
    near_r,
    far_s,
    far_r,
    pack_s,
    pack_rs,
    cols_s,
    cols_r,
    ready,
):
    vi = lax.axis_index("views")
    cj = lax.axis_index("cols")
    odd = lax.rem(vi, 2)
    even = 1 - odd
    partner = vi + 1 - 2 * odd
    ahead = lax.rem(vi + nv + 2 - 4 * odd, nv)
    behind = lax.rem(vi + nv - 2 + 4 * odd, nv)
    left = lax.rem(cj + nc - 1, nc)
    right = lax.rem(cj + 1, nc)
    at_top = vi == 0
    at_bottom = vi == nv - 1
    has_far = jnp.logical_and(vi > 0, vi < nv - 1)
    sends_far = jnp.logical_and(vi != nv - 2, vi != 1)

    barrier = pltpu.get_barrier_semaphore()
    has_left, has_right = cj > 0, cj < nc - 1

    def greet(there):
        pl.semaphore_signal(barrier, inc=1, device_id=there, device_id_type=MESH)

    middle = nc // 2
    is_even = lax.rem(cj, 2) == 0
    late_l = jnp.logical_and(has_left, jnp.logical_and(is_even, cj != middle))
    late_r = jnp.logical_and(has_right, jnp.logical_or(is_even, cj == middle - 1))
    early_l = jnp.logical_and(has_left, jnp.logical_not(late_l))
    early_r = jnp.logical_and(has_right, jnp.logical_not(late_r))
    late_z = jnp.logical_and(has_far, odd == 0)
    early_z = jnp.logical_and(sends_far, odd == 0)
    late_q = jnp.logical_and(sends_far, odd == 1)
    early_q = jnp.logical_and(has_far, odd == 1)

    greet((partner, cj))
    for exists, there in (
        (early_z, (ahead, cj)),
        (early_q, (behind, cj)),
        (early_l, (vi, left)),
        (early_r, (vi, right)),
    ):

        @pl.when(exists)
        def _():
            greet(there)

    load = pltpu.make_async_copy(f_hbm, fv, load_sem)
    load.start()

    def remote(src, dst, s, r, there):
        return pltpu.make_async_remote_copy(
            src_ref=src, dst_ref=dst, send_sem=s, recv_sem=r, device_id=there, device_id_type=MESH
        )

    def near(k):
        span = pl.ds(k * CHUNK, CHUNK)
        return remote(f_hbm.at[:, span], got.at[odd, :, span], near_s, near_r.at[k], (partner, cj))

    def near_in(k):
        span = pl.ds(k * CHUNK, CHUNK)
        return remote(f_hbm.at[:, span], got.at[even, :, span], near_s, near_r.at[k], (partner, cj))

    def far(k):
        span = pl.ds(k * CHUNK, CHUNK)
        return remote(got.at[even, :, span], got.at[odd, :, span], far_s, far_r.at[k // 2], (ahead, cj))

    to_left = remote(pack_out.at[0], pack_r, pack_s.at[0], pack_rs.at[0], (vi, left))
    to_right = remote(pack_out.at[1], pack_l, pack_s.at[1], pack_rs.at[1], (vi, right))

    load.wait()

    row8 = lax.broadcasted_iota(jnp.int32, (8, PLANE), 0)
    row16 = lax.broadcasted_iota(jnp.int32, (16, X), 0)
    lane16 = lax.broadcasted_iota(jnp.int32, (16, X), 1)
    r8 = lax.rem(row16, 8)
    wanted = jnp.where(r8 < 4, r8 + (X - 4), r8 - 4)

    packed = jnp.zeros((16, PLANE), F32)
    for u in range(ROWS):
        pick = jnp.where(jnp.logical_and(lane16 == wanted, row16 // 8 == u), 1.0, 0.0).astype(BF16)
        packed = packed + lax.dot_general(
            pick, fv[u].reshape(PLANE, X), (((1,), (1,)), ((), ())), preferred_element_type=F32
        )
    pack[...] = packed.astype(BF16)

    def folded(a):
        return jnp.concatenate([a[:, : PLANE // 2], a[:, PLANE // 2 :]], axis=0).astype(BF16)

    def unfolded(a):
        a = a.astype(F32)
        return jnp.concatenate([a[:8], a[8:]], axis=1)

    pack_out[0] = folded(jnp.where(row8 < 4, pltpu.roll(packed[:8], 4, 0), packed[8:]))
    pack_out[1] = folded(jnp.where(row8 < 4, packed[:8], pltpu.roll(packed[8:], 4, 0)))
    four = jnp.where(row8 < 4, pltpu.roll(packed[:8], 6, 0), pltpu.roll(packed[8:], 2, 0))
    own_cols[...] = folded(four)

    greeted = jnp.int32(1)
    for late in (late_z, late_q, late_l, late_r):
        greeted = greeted + jnp.where(late, 1, 0)
    pl.semaphore_wait(barrier, greeted)

    def tell(which, there):
        pl.semaphore_signal(ready.at[which], inc=1, device_id=there, device_id_type=MESH)

    @pl.when(late_l)
    def _():
        to_left.start()
        tell(1, (vi, left))

    @pl.when(late_r)
    def _():
        to_right.start()
        tell(0, (vi, right))

    @pl.when(late_z)
    def _():
        tell(2, (behind, cj))

    cols_near = remote(own_cols, cols_in.at[1, odd], cols_s.at[0], cols_r.at[0], (partner, cj))
    cols_far = remote(cols_in.at[1, even], cols_in.at[1, odd], cols_s.at[1], cols_r.at[1], (ahead, cj))
    cols_near.start()
    for k in range(FIRST):
        near(k).start()

    held = jnp.logical_or(cj == nc // 2 - 1, cj == nc // 2)

    @pl.when(jnp.logical_not(held))
    def _():
        for k in range(FIRST, CHUNKS):
            near(k).start()

    def passed(far_too, slot):
        return (
            remote(
                cols_in.at[1, slot],
                cols_in.at[2, slot],
                cols_s.at[2 + far_too],
                cols_r.at[2 + far_too],
                (vi, left),
            ),
            remote(
                cols_in.at[1, slot],
                cols_in.at[0, slot],
                cols_s.at[4 + far_too],
                cols_r.at[4 + far_too],
                (vi, right),
            ),
        )

    near_left, near_right = passed(0, even)
    far_left, far_right = passed(1, odd)

    @pl.when(at_top)
    def _():
        got[0, 0] = fv[0]
        got[0, 1] = jnp.zeros((V, Y, X), BF16)

    @pl.when(at_bottom)
    def _():
        got[1, 0] = jnp.zeros((V, Y, X), BF16)
        got[1, 1] = fv[1]

    def lanes(a, k):
        return pltpu.roll(a, (-k) % a.shape[-1], a.ndim - 1)

    def smooth_lanes(a):
        pair = a + lanes(a, -1)
        return pair + lanes(pair, 1)

    def horizontal(i, carry):
        before, last = carry
        u = i // H_STEPS
        v0 = lax.rem(i, H_STEPS) * H_CHUNK
        top = v0 == 0
        before = [jnp.where(top, 0.0, c) for c in before]
        last = [jnp.where(top, 0.0, c) for c in last]
        here = fv[u, pl.ds(v0, H_CHUNK)].astype(F32)
        full[u, pl.ds(v0, H_CHUNK)] = here
        above = jnp.where(top, 0.0, fv[u, jnp.maximum(v0 - 1, 0)].astype(F32))
        below = jnp.where(
            v0 + H_CHUNK < V, fv[u, jnp.minimum(v0 + H_CHUNK, V - 1)].astype(F32), 0.0
        )
        mid_x = jnp.concatenate([above[None], here, below[None]], 0)
        left_x, right_x = lanes(mid_x, -1), lanes(mid_x, 1)
        grad_v = [a[2:] - a[:-2] for a in (left_x, mid_x, right_x)]
        grad_x = [here - lanes(here, -2), right_x[1:-1] - left_x[1:-1], lanes(here, 2) - here]

        def smooth_x(p, q):
            a, b, c = (s * t for s, t in zip(p, q))
            return (a + c) + (b + b)

        now = [smooth_x(grad_v, grad_v), smooth_x(grad_v, grad_x), smooth_x(grad_x, grad_x)]
        run = [jnp.concatenate([a[None], b[None], c], 0) for a, b, c in zip(before, last, now)]
        pairs = [c[1:] + c[:-1] for c in run]
        w, m = weighted(*(c[1:] + c[:-1] for c in pairs))
        weight[u, pl.ds(v0, H_CHUNK)] = w
        moment[u, pl.ds(v0, H_CHUNK)] = m

        @pl.when(v0 == V - H_CHUNK)
        def _():
            w, m = weighted(*(c[-1] + d[-1] for c, d in zip(pairs, now)))
            weight[u, V] = w
            moment[u, V] = m

        return [c[H_CHUNK - 2] for c in now], [c[H_CHUNK - 1] for c in now]

    zeros = [jnp.zeros((Y, X), F32)] * 3
    lax.fori_loop(0, 2 * H_STEPS, horizontal, (zeros, zeros))

    @pl.when(early_l)
    def _():
        pl.semaphore_wait(ready.at[0], 1)
        to_left.start()

    @pl.when(early_r)
    def _():
        pl.semaphore_wait(ready.at[1], 1)
        to_right.start()

    @pl.when(early_z)
    def _():
        pl.semaphore_wait(ready.at[2], 1)

    cols_near.wait_recv()

    @pl.when(sends_far)
    def _():
        cols_far.start()

    @pl.when(has_left)
    def _():
        near_left.start()

    @pl.when(has_right)
    def _():
        near_right.start()

    @pl.when(held)
    def _():
        for k in range(FIRST, SECOND):
            near(k).start()

    def relay(k):
        near_in(k).wait_recv()

        @pl.when(sends_far)
        def _():
            far(k).start()


    lane = lax.broadcasted_iota(jnp.int32, (STEP, Y, X), 2)
    sub = lax.broadcasted_iota(jnp.int32, (STEP, Y, X), 1)
    rim = jnp.logical_or(lane < 2, lane >= X - 2)
    outer = jnp.logical_or(lane == 0, lane == X - 1)

    def parts(ref, *at):
        return [ref[at]]

    def y_up(a, rest=0.0):
        return [jnp.where(sub == Y - 1, rest, pltpu.roll(a[0], Y - 1, 1))]

    def y_down(a):
        return [jnp.where(sub == 0, 0.0, pltpu.roll(a[0], 1, 1))]

    def smooth_y(a):
        pair = [b + c for b, c in zip(a, y_down(a))]
        return [b + c for b, c in zip(pair, y_up(pair, a[0]))]

    def vertical(v0):
        span = pl.ds(v0, STEP)
        for slot in range(2):
            for u in range(ROWS):
                wide[2 * slot + u] = got[slot, u, span].astype(F32)
        every = slice(None)
        field = (
            [parts(wide, 0, every), parts(wide, 1, every)]
            + [parts(full, u, span) for u in range(ROWS)]
            + [parts(wide, 2, every), parts(wide, 3, every)]
        )
        comps = []
        for r in range(1, 5):
            grad_u = [a - b for a, b in zip(field[r + 1], field[r - 1])]
            grad_y = [a - b for a, b in zip(y_up(field[r]), y_down(field[r]))]
            comps.append(
                [
                    [a * b for a, b in zip(g, h)]
                    for g, h in ((grad_u, grad_u), (grad_u, grad_y), (grad_y, grad_y))
                ]
            )
        pairs = [
            [[a + b for a, b in zip(c, d)] for c, d in zip(comps[r], comps[r + 1])] for r in range(3)
        ]
        for u in range(ROWS):
            tensor = [
                smooth_y([a + b for a, b in zip(c, d)]) for c, d in zip(pairs[u], pairs[u + 1])
            ]
            past = pl.ds(v0 + 1, STEP)
            w, m = parts(weight, u, past), parts(moment, u, past)
            slope[u, span] = join(w[0], m[0], *(c[0] for c in tensor))

    def variation(v0):
        span = pl.ds(v0, STEP)
        for u in range(ROWS):
            t = parts(fix, u, span)
            joined = [jnp.where(rim, t[0], slope[u, span])]
            flux_x, flux_y = [], []
            for here, below in zip(joined, y_up(joined)):
                step_x = lanes(here, 1) - here
                step_y = below - here
                scale = lax.rsqrt(step_x * step_x + step_y * step_y + 1.0)
                flux_x.append(step_x * scale)
                flux_y.append(step_y * scale)
            for p, above in enumerate(y_down(flux_y)):
                depth = joined[p] + 0.2 * (flux_x[p] - lanes(flux_x[p], -1) + flux_y[p] - above)
                out[u, span] = jnp.where(outer, lanes(t[p], -63), depth)

    place = lax.broadcasted_iota(jnp.int32, (8, PLANE), 1)
    y_at = lax.rem(place, Y)

    def cols_by(a, k):
        return pltpu.roll(a, (-k) % 8, 0)

    def y_by(a, k):
        return jnp.where(y_at == (Y - 1 if k > 0 else 0), 0.0, pltpu.roll(a, (-k) % PLANE, 1))

    def v_by(a, k):
        return jnp.where(
            place >= PLANE - Y if k > 0 else place < Y, 0.0, pltpu.roll(a, (-k * Y) % PLANE, 1)
        )

    def smooth_by(by, a):
        return by(a, -1) + (a + a) + by(a, 1)

    for k in range(4):
        relay(k)

    @pl.when(has_far)
    def _():
        cols_far.wait_recv()

        @pl.when(has_left)
        def _():
            far_left.start()

        @pl.when(has_right)
        def _():
            far_right.start()

    @pl.when(held)
    def _():
        for k in range(SECOND, CHUNKS):
            near(k).start()

    relay(4)
    @pl.when(has_left)
    def _():
        to_right.wait_recv()

    @pl.when(has_right)
    def _():
        to_left.wait_recv()

    first, final = cj == 0, cj == nc - 1
    own = pack[...].astype(F32)
    from_l = unfolded(pack_l[...])
    from_r = unfolded(pack_r[...])
    for u in range(ROWS):
        mine = own[8 * u : 8 * u + 8]
        l_in = pltpu.roll(from_l, 4, 0) if u else from_l
        r_in = from_r if u else pltpu.roll(from_r, 4, 0)
        flip_l = jnp.where(row8 == 2, pltpu.roll(mine, 6, 0), 0.0)
        flip_r = jnp.where(row8 == 5, pltpu.roll(mine, 2, 0), 0.0)
        l_in = jnp.where(first, flip_l, l_in)
        r_in = jnp.where(final, flip_r, r_in)
        e_l = jnp.where(row8 < 4, l_in, mine)
        e_r = jnp.where(row8 < 4, mine, r_in)
        edge[0, 2 + u] = e_l
        edge[1, 2 + u] = e_r

    def edges_h(side, carry):
        for u in range(ROWS):
            f = edge[side, 2 + u]
            grad_v = v_by(f, 1) - v_by(f, -1)
            grad_x = cols_by(f, 1) - cols_by(f, -1)
            w, m = weighted(
                *(
                    smooth_by(v_by, smooth_by(cols_by, c))
                    for c in (grad_v * grad_v, grad_v * grad_x, grad_x * grad_x)
                )
            )
            edge_j[side, u] = w
            edge_d[side, u] = m
        relay(5 + side)
        return carry

    lax.fori_loop(0, 2, edges_h, 0)


    def arrived(g):
        @pl.when(has_far)
        def _():
            both = pl.ds(g * STEP, STEP)
            remote(
                got.at[even, :, both], got.at[odd, :, both], far_s, far_r.at[g], (ahead, cj)
            ).wait_recv()

    def start(g, carry):
        @pl.when(g > 0)
        def _():
            relay(2 * g + 6)

        relay(2 * g + 7)
        arrived(g)
        vertical(g * STEP)
        return carry

    lax.fori_loop(0, BEFORE, start, 0)

    @pl.when(has_left)
    def _():
        near_right.wait_recv()

        @pl.when(has_far)
        def _():
            far_right.wait_recv()

    @pl.when(has_right)
    def _():
        near_left.wait_recv()

        @pl.when(has_far)
        def _():
            far_left.wait_recv()

    for slot in range(2):
        from_l, here, from_r = (
            unfolded(cols_in[origin, slot]) for origin in range(3)
        )
        for u in range(ROWS):
            with_l = jnp.where(row8 == 4 * u + 1, from_l, here)
            with_r = jnp.where(row8 == 4 * u + 2, from_r, here)
            edge[0, 4 * slot + u] = pltpu.roll(with_l, 2 + 4 * u, 0)
            edge[1, 4 * slot + u] = pltpu.roll(with_r, 2 + 4 * u, 0)

    @pl.when(at_top)
    def _():
        for side in range(2):
            edge[side, 0] = edge[side, 2]
            edge[side, 1] = jnp.zeros((8, PLANE), F32)

    @pl.when(at_bottom)
    def _():
        for side in range(2):
            edge[side, 4] = jnp.zeros((8, PLANE), F32)
            edge[side, 5] = edge[side, 3]

    def edges(side, carry):
        relay(2 * BEFORE + 6 + side)
        j_below = jnp.where(jnp.logical_and(final, side == 1), 4, 8)
        q_from = jnp.where(jnp.logical_and(first, side == 0), 4, 0)
        tiles = [edge[side, r] for r in range(6)]
        comps = []
        for r in range(1, 5):
            grad_u = tiles[r + 1] - tiles[r - 1]
            grad_y = y_by(tiles[r], 1) - y_by(tiles[r], -1)
            comps.append((grad_u * grad_u, grad_u * grad_y, grad_y * grad_y))
        for u in range(ROWS):
            w, m = edge_j[side, u], edge_d[side, u]
            tensor = [
                smooth_by(y_by, a + (b + b) + c) for a, b, c in zip(comps[u], comps[u + 1], comps[u + 2])
            ]
            joined = jnp.where(row8 < j_below, join(w, m, *tensor), 0.0)
            step_x = cols_by(joined, 1) - joined
            step_y = y_by(joined, 1) - joined
            scale = lax.rsqrt(step_x * step_x + step_y * step_y + 1.0)
            flux_x = jnp.where(row8 >= q_from, step_x * scale, 0.0)
            flux_y = step_y * scale
            depth = joined + 0.2 * (flux_x - cols_by(flux_x, -1) + flux_y - y_by(flux_y, -1))
            edge_j[side, u] = pltpu.roll(joined, 4, 0)
            edge_d[side, u] = pltpu.roll(depth, 5, 0)
        return carry

    lax.fori_loop(0, 2, edges, 0)

    small = lax.broadcasted_iota(jnp.int32, (8, X), 0)

    def spread_out(u, carry):
        for b in range(PLANE // X):
            part = pl.ds(b * X, X)
            both = jnp.where(small == 0, edge_d[1, u, :, part], edge_d[0, u, :, part])
            block = jnp.concatenate(
                [
                    edge_j[0, u, :, part],
                    jnp.zeros((56, X), F32),
                    both,
                    jnp.zeros((48, X), F32),
                    edge_j[1, u, :, part],
                ],
                axis=0,
            )
            fix[u, pl.ds(4 * b, 4)] = block.T.reshape(4, Y, X)
        return carry

    relay(2 * BEFORE + 8)
    lax.fori_loop(0, 2, spread_out, 0)

    def finish(g, carry):
        for k in range(2):

            @pl.when(2 * g + k + 9 < CHUNKS)
            def _():
                relay(2 * g + k + 9)

        def varied(i, c):
            variation(i * STEP)
            return c

        lax.fori_loop(jnp.where(g == BEFORE, 0, g - 1), g, varied, 0)
        arrived(g)
        vertical(g * STEP)
        return carry

    lax.fori_loop(BEFORE, V // STEP, finish, 0)
    variation(V - STEP)

    @pl.when(has_left)
    def _():
        to_left.wait_send()
        near_left.wait_send()

    @pl.when(has_right)
    def _():
        to_right.wait_send()
        near_right.wait_send()

    @pl.when(jnp.logical_and(has_left, has_far))
    def _():
        far_left.wait_send()

    @pl.when(jnp.logical_and(has_right, has_far))
    def _():
        far_right.wait_send()

    cols_near.wait_send()
    remote(f_hbm, got.at[odd], near_s, near_r.at[0], (partner, cj)).wait_send()

    @pl.when(sends_far)
    def _():
        cols_far.wait_send()
        remote(got.at[even], got.at[odd], far_s, far_r.at[0], (ahead, cj)).wait_send()


def local(nv, nc, light_field):
    block = (ROWS, V, Y, X)
    dma = pltpu.SemaphoreType.DMA
    return pl.pallas_call(
        functools.partial(kernel, nv, nc),
        out_shape=jax.ShapeDtypeStruct(block, F32),
        in_specs=[pl.BlockSpec(memory_space=pl.ANY)],
        out_specs=pl.BlockSpec(memory_space=pltpu.VMEM),
        scratch_shapes=[
            pltpu.VMEM(block, BF16),
            pltpu.VMEM(block, F32),
            pltpu.VMEM((2, *block), BF16),
            pltpu.VMEM((4, STEP, Y, X), F32),
            pltpu.VMEM((ROWS, V + 1, Y, X), F32),
            pltpu.VMEM((ROWS, V + 1, Y, X), F32),
            pltpu.VMEM(block, F32),
            pltpu.VMEM(block, F32),
            pltpu.VMEM((16, PLANE), BF16),
            pltpu.VMEM((2, 16, PLANE // 2), BF16),
            pltpu.VMEM((16, PLANE // 2), BF16),
            pltpu.VMEM((16, PLANE // 2), BF16),
            pltpu.VMEM((16, PLANE // 2), BF16),
            pltpu.VMEM((3, 2, 16, PLANE // 2), BF16),
            pltpu.VMEM((2, 6, 8, PLANE), F32),
            pltpu.VMEM((2, ROWS, 8, PLANE), F32),
            pltpu.VMEM((2, ROWS, 8, PLANE), F32),
            dma,
            dma,
            dma((CHUNKS,)),
            dma,
            dma((CHUNKS // 2,)),
            dma((2,)),
            dma((2,)),
            dma((6,)),
            dma((6,)),
            pltpu.SemaphoreType.REGULAR((3,)),
        ],
        compiler_params=pltpu.CompilerParams(
            collective_id=0, has_side_effects=True, vmem_limit_bytes=32 << 20
        ),
        cost_estimate=pl.CostEstimate(flops=60_000_000, bytes_accessed=1_600_000, transcendentals=800_000),
    )(pltpu.with_memory_space_constraint(light_field, pltpu.HBM))


def solution(mesh):
    return jax.shard_map(
        functools.partial(local, mesh.shape["views"], mesh.shape["cols"]),
        mesh=mesh,
        in_specs=(P("views", None, None, "cols"),),
        out_specs=P("views", None, None, "cols"),
        check_vma=False,
    )
```
